128 devices in a mesh: slab: 16 (over x, y), group: 8 (over z, core).
Axes of the slice: x: 4, y: 4, z: 4, core: 2. Of those that a mesh axis runs over, the one named last changes fastest.
Arguments:
- disp_now: float32 [3, 524288], P(None, 'slab'), may hold values from -6 to 6
- disp_prev: float32 [3, 524288], P(None, 'slab'), may hold values from -6 to 6
- inv_mass: float32 [524288], P('slab'), may hold values from 0.5 to 2
- cell_nodes: int32 [4096, 192], P(('slab', 'group')), may hold values from 0 to 98303
- shape_grads: bfloat16 [4096, 3, 192, 128], P(('slab', 'group')), may hold values from -0.125 to 0.125
- cell_weights: float32 [4096, 128], P(('slab', 'group')), may hold values from 0.5 to 2
- cell_shear: float32 [4096], P(('slab', 'group')), may hold values from 0.5 to 2
- cell_bulk: float32 [4096], P(('slab', 'group')), may hold values from 1 to 4
- block_owner: int32 [4096, 1], P(('slab', 'group')), may hold values from 0 to 15; in each aligned block of 32 rows (0 to 31, 32 to 63, ...) at most 4 rows name the same one
- block_nodes: int32 [4096, 256], P(('slab', 'group')), may hold values from 0 to 32767
- block_phi: float32 [4096, 128, 256], P(('slab', 'group')), may hold values from -0.375 to 0.375
- block_corr: float32 [4096, 128, 128], P(('slab', 'group')), may hold values from -0.5 to 0.5
- block_target: float32 [4096, 3, 128], P(('slab', 'group')), may hold values from -6 to 6
- block_fixed: int32 [4096, 128], P(('slab', 'group')), may hold values 0 or 1
Outputs:
- disp_final: float32 [3, 524288], P(None, 'slab')
The draws below stay inside these ranges and needn't reach their ends.
Inputs may be any that keep to these rules, and one draw needn't show every extreme that they name: `cell_nodes`: support node numbers run over the slab below, the cell's own slab and the slab above; those outside the head read zero. `block_owner`: among the 32 blocks of one device at most 4 have one owner slab, and in every draw some device has exactly 4 with one owner.
All inputs are finite; a program needn't handle non-finite values. No bound on the sum of `block_fixed` on one device may be relied on, other than what follows from the above.
Results may differ from the reference program's by a relative error of at most 0.0059.
Values may be sent and summed in bfloat16 or wider, within the bound.
A program may use at most 192 MiB of HBM per device.

```python
import math
import jax
import jax.numpy as jnp
import numpy as np
from jax import lax

NODE_SLAB = 32768
CELL_DEV = 32
PTS = 128
SUP = 192
BLK_DEV = 32
CAP = 4
BN = 128
BSUP = 256
SLABS = 16
NODES = 524288
CELLS = 4096
BLOCKS = 4096
N_SLAB = 16
N_GROUP = 8


def plant(values, own_key, low, top_value):
    longest = values.shape.index(max(values.shape))
    spots = []
    for shift in (0, 1):
        where = [jax.random.randint(jax.random.fold_in(own_key, axis), (), 0, length) for axis, length in enumerate(values.shape)]
        where[longest] = (where[longest] + shift) % values.shape[longest]
        spots.append(tuple(where))
    return values.at[spots[0]].set(low).at[spots[1]].set(top_value)


def block_levels(key, dims, split, low, top_value):
    factor_of, own = 1.0, jax.random.fold_in(key, 6)
    for dim, shards_of in split:
        heights = jnp.exp(jax.random.uniform(jax.random.fold_in(own, dim), (shards_of,), jnp.float32, low / len(split), top_value / len(split)))
        factor_of = factor_of * jnp.repeat(heights, dims[dim] // shards_of).reshape([-1 if axis == dim else 1 for axis in range(len(dims))])
    return factor_of


def deal_out(stream_key, own, number, rows, count, top, limit, slope):
    sequence = jax.random.permutation(stream_key, count)
    packed, usual = portions_of(count, rows * top, limit, slope, True), portions_of(count, rows * top, limit, slope, False)
    places = jnp.arange(count)

    def named(lengths, turn):
        used = int((lengths > 0).sum())
        fixed = max(1, used // 4)
        moved = fixed + (places - fixed + turn * (used - fixed)) % max(1, count - fixed)
        return jnp.zeros((count,), jnp.int32).at[sequence[jnp.where(places < fixed, places, moved)]].set(jnp.asarray(lengths, jnp.int32))

    lengths = jnp.where(number % 4 == 0, named(packed, number // 4), named(usual, number - number // 4 - 1))
    mixed = jax.random.permutation(jax.random.fold_in(own, 3), count)
    giver, sink = mixed[0:count // 2 * 2:2], mixed[1:count // 2 * 2:2]
    margin = jnp.minimum(lengths[giver] - 1, limit - lengths[sink]) // 2
    margin = jnp.where((giver == sequence[0]) | (sink == sequence[0]) | (lengths[sink] == 0), 0, jnp.maximum(margin, 0))
    moved = jax.random.randint(jax.random.fold_in(own, 4), (count // 2,), 0, 1 << 20) % (margin + 1)
    lengths = lengths.at[giver].add(-moved).at[sink].add(moved)
    labels = jnp.searchsorted(jnp.cumsum(lengths), jnp.arange(rows * top), side="right").astype(jnp.int32)
    table = labels.reshape(top, rows).T
    table = table[jax.random.permutation(jax.random.fold_in(own, 1), rows)]
    turn = jax.random.randint(jax.random.fold_in(own, 2), (rows, 1), 0, top)
    return jnp.take_along_axis(table, (jnp.arange(top)[None, :] + turn) % top, axis=1)


def portions_of(count, total, limit, skew, full):
    portions = [(1 << 20) // math.isqrt(grade ** skew) + 1 for grade in range(1, count + 1)]
    largest = limit if full else min(limit, max(-(-total // count), total * portions[0] // sum(portions)))
    least = 1 if total - largest >= count - 1 else 0
    given, rest = [largest] + [least] * (count - 1), total - largest - least * (count - 1)
    while rest > 0:
        free = [i for i in range(1, count) if given[i] < largest] or [i for i in range(1, count) if given[i] < limit]
        whole, left = sum([portions[i] for i in free]), rest
        for i in free:
            addition = min(limit - given[i], max(1, left * portions[i] // whole), rest)
            given[i] = given[i] + addition
            rest = rest - addition
    return np.array(given)


def normal_values(own_key, shape, deviation, bound, pieces=(), kind=jnp.bfloat16):
    result = deviation * jax.random.normal(own_key, shape, jnp.float32)
    if pieces:
        result = result * block_levels(own_key, shape, pieces, -0.22, 0.18)
    return jnp.clip(result, -bound, bound).astype(kind)


def setup_inputs(seed: int = 0) -> dict:
    seeds = jax.random.split(jax.random.key(seed), 15)
    disp_now = normal_values(seeds[0], (3, NODES), 1.0, 6.0, ((1, 16),), jnp.float32)
    disp_prev = normal_values(seeds[1], (3, NODES), 1.0, 6.0, ((1, 16),), jnp.float32)
    inv_mass = jnp.clip(jnp.exp(math.log(2.0) - 1.3862944 * jax.random.uniform(seeds[2], (NODES,), jnp.float32) ** block_levels(seeds[2], (NODES,), ((0, 16),), -0.2, 0.2)), 0.5, 2.0)
    cell_nodes = plant(jax.random.randint(seeds[3], (CELLS, SUP), 0, 3 * NODE_SLAB), jax.random.fold_in(seeds[3], 1), 0, (3 * NODE_SLAB) - 1).astype(jnp.int32)
    shape_grads = normal_values(seeds[4], (CELLS, 3, SUP, PTS), (SUP * 11) ** -0.5, 0.125, ((0, 128),))
    cell_weights = jnp.clip(jnp.exp(math.log(2.0) - 1.3862944 * jax.random.uniform(seeds[5], (CELLS, PTS), jnp.float32) ** block_levels(seeds[5], (CELLS, PTS), ((0, 128),), -0.2, 0.2)), 0.5, 2.0)
    cell_shear = jnp.clip(jnp.exp(math.log(2.0) - 1.3862944 * jax.random.uniform(seeds[6], (CELLS,), jnp.float32) ** block_levels(seeds[6], (CELLS,), ((0, 128),), -0.2, 0.2)), 0.5, 2.0)
    cell_bulk = jnp.clip(jnp.exp(math.log(4.0) - 1.3862944 * jax.random.uniform(seeds[7], (CELLS,), jnp.float32) ** block_levels(seeds[7], (CELLS,), ((0, 128),), -0.2, 0.2)), 1.0, 4.0)
    block_owner_keys = jax.random.split(jax.random.fold_in(seeds[8], 1), BLOCKS // BLK_DEV)
    block_owner_turns = jax.random.permutation(jax.random.fold_in(seeds[8], 3), BLOCKS // BLK_DEV)
    block_owner = jax.vmap(lambda own, number: deal_out(jax.random.fold_in(seeds[8], 2), own, number, BLK_DEV, SLABS, 1, CAP, 2))(block_owner_keys, block_owner_turns).reshape((BLOCKS, 1))
    block_nodes = plant(jax.random.randint(seeds[9], (BLOCKS, BSUP), 0, NODE_SLAB), jax.random.fold_in(seeds[9], 1), 0, NODE_SLAB - 1).astype(jnp.int32)
    block_phi = normal_values(seeds[10], (BLOCKS, BN, BSUP), BSUP ** -0.5, 0.375, ((0, 128),), jnp.float32)
    block_corr = normal_values(seeds[11], (BLOCKS, BN, BN), BN ** -0.5, 0.5, ((0, 128),), jnp.float32)
    block_target = normal_values(seeds[12], (BLOCKS, 3, BN), 1.0, 6.0, ((0, 128),), jnp.float32)
    block_fixed = plant((jax.random.randint(seeds[13], (BLOCKS, BN), 0, 2) < 1).astype(jnp.int32), jax.random.fold_in(seeds[13], 1), 0, 1)
    return dict(disp_now=disp_now, disp_prev=disp_prev, inv_mass=inv_mass, cell_nodes=cell_nodes, shape_grads=shape_grads, cell_weights=cell_weights, cell_shear=cell_shear, cell_bulk=cell_bulk, block_owner=block_owner, block_nodes=block_nodes, block_phi=block_phi, block_corr=block_corr, block_target=block_target, block_fixed=block_fixed)


def stress_of(grad, shear, bulk):
    identity = jnp.eye(3, dtype=grad.dtype)
    full = grad + identity[None, :, :, None]
    entries = [[full[:, leading, trailing] for trailing in range(3)] for leading in range(3)]
    cofactor = [[entries[(leading + 1) % 3][(trailing + 1) % 3] * entries[(leading + 2) % 3][(trailing + 2) % 3]
                 - entries[(leading + 1) % 3][(trailing + 2) % 3] * entries[(leading + 2) % 3][(trailing + 1) % 3]
                 for trailing in range(3)] for leading in range(3)]
    volume = entries[0][0] * cofactor[0][0] + entries[0][1] * cofactor[0][1] + entries[0][2] * cofactor[0][2]
    clamped = jnp.maximum(volume, 0.3)
    shear_now = shear[:, None]
    factor = (bulk[:, None] * jnp.log(clamped) - shear_now) / clamped
    rows_out = [jnp.stack([shear_now * entries[leading][trailing] + factor * cofactor[leading][trailing]
                           for trailing in range(3)], axis=1) for leading in range(3)]
    return jnp.stack(rows_out, axis=1)


def reference(disp_now, disp_prev, inv_mass, cell_nodes, shape_grads, cell_weights, cell_shear, cell_bulk,
              block_owner, block_nodes, block_phi, block_corr, block_target, block_fixed):
    width = NODE_SLAB
    padded = jnp.pad(disp_now.astype(jnp.bfloat16), ((0, 0), (width, width)))
    per_slab = CELL_DEV * N_GROUP

    def one_slab(total, inputs):
        position, nodes, grads, weights, shear, bulk = inputs
        global_index = (nodes + position * width).astype(jnp.int32)
        gathered = jnp.moveaxis(jnp.take(padded, global_index, axis=1), 0, 1)
        grad = jnp.einsum('cia,cjap->cijp', gathered.astype(jnp.float32), grads.astype(jnp.float32))
        stress = stress_of(grad, shear, bulk)
        weighted = (weights[:, None, None, :] * stress).astype(jnp.bfloat16)
        force = jnp.einsum('cijp,cjap->cia', weighted.astype(jnp.float32), grads.astype(jnp.float32))
        total = total.at[:, global_index].add(jnp.moveaxis(force, 1, 0))
        return total, None

    inputs = (jnp.arange(N_SLAB, dtype=jnp.int32),
              cell_nodes.reshape(N_SLAB, per_slab, SUP),
              shape_grads.reshape((N_SLAB, per_slab) + shape_grads.shape[1:]),
              cell_weights.reshape(N_SLAB, per_slab, PTS),
              cell_shear.reshape(N_SLAB, per_slab),
              cell_bulk.reshape(N_SLAB, per_slab))
    start = jnp.zeros((3, NODES + 2 * width), jnp.float32)
    total, _ = lax.scan(one_slab, start, inputs)
    force_sum = total[:, width:width + NODES]
    disp_next = 2.0 * disp_now - disp_prev - inv_mass[None, :] * force_sum

    block_index = (block_owner[:, 0:1] * width + block_nodes).astype(jnp.int32)
    values = jnp.moveaxis(jnp.take(disp_next, block_index, axis=1), 0, 1)
    highest = lax.Precision.HIGHEST
    interp = jnp.einsum('bma,bia->bim', block_phi, values, precision=highest)
    resid = block_fixed[:, None, :].astype(jnp.float32) * (block_target - interp)
    corr = jnp.einsum('bmq,biq->bim', block_corr, resid, precision=highest)
    delta = jnp.einsum('bma,bim->bia', block_phi, corr, precision=highest)
    added = jnp.zeros((3, NODES), jnp.float32).at[:, block_index].add(jnp.moveaxis(delta, 1, 0))
    return disp_next + added
```

```python
import jax
import jax.numpy as jnp
from jax import lax
from jax.experimental import pallas as pl
from jax.experimental.pallas import tpu as pltpu
from jax.sharding import PartitionSpec as P

BF = jnp.bfloat16
F32 = jnp.float32
NT = (((1,), (1,)), ((), ()))
MESH = pl.DeviceIdType.MESH
CAP = 4
QUAD = 768


def onehot(index, size):
    rows = lax.broadcasted_iota(jnp.int32, (size, index.shape[1]), 0)
    return jnp.where(rows == index, 1.0, 0.0).astype(BF)


def cells_kernel(nodes, table, weights, shear, bulk, grads_hbm, out, grads, field, near, columns, spread, sem):
    load = pltpu.make_async_copy(grads_hbm, grads, sem)
    load.start()
    rows_of = lax.broadcasted_iota(jnp.int32, (128, QUAD), 0)

    def gather(quad, carry):
        node = nodes[quad]
        slab, row, column = node >> 15, (node >> 8) & 127, node & 255
        total = None
        for side in range(3):
            hot = onehot(jnp.where(slab == side, column, -1), 256)
            columns[quad, side] = hot
            part = jnp.dot(table[side], hot, preferred_element_type=F32)
            total = part if total is None else total + part
        mask = rows_of == row
        for i in range(3):
            near[quad, i : i + 1, :] = jnp.sum(
                jnp.where(mask, total[128 * i : 128 * i + 128], 0.0), axis=0, keepdims=True
            )
        return carry

    lax.fori_loop(0, 8, gather, 0)
    load.wait()
    sub = lax.broadcasted_iota(jnp.int32, (8, 384), 0)
    lane = lax.broadcasted_iota(jnp.int32, (8, 384), 1)
    own = (sub >= 4) == (lane >= 192)

    def gradient(quad, carry):
        for pair in range(2):
            left = jnp.zeros((8, 384), F32)
            for i in range(3):
                left = jnp.where(sub % 4 == i, near[quad, i : i + 1, 384 * pair : 384 * pair + 384], left)
            left = jnp.where(own, left, 0.0).astype(BF)
            for j in range(3):
                first = 4 * quad + 2 * pair
                both = jnp.concatenate([grads[first, j], grads[first + 1, j]], axis=0)
                at = pl.ds(pl.multiple_of(16 * quad + 8 * pair, 8), 8)
                field[j, at, :] = jnp.dot(left, both, preferred_element_type=F32)
        return carry

    lax.fori_loop(0, 8, gradient, 0)
    full = [
        [field[j, pl.ds(i, 32, stride=4), :] + (1.0 if i == j else 0.0) for j in range(3)]
        for i in range(3)
    ]
    cofactor = [
        [
            full[(i + 1) % 3][(j + 1) % 3] * full[(i + 2) % 3][(j + 2) % 3]
            - full[(i + 1) % 3][(j + 2) % 3] * full[(i + 2) % 3][(j + 1) % 3]
            for j in range(3)
        ]
        for i in range(3)
    ]
    volume = full[0][0] * cofactor[0][0] + full[0][1] * cofactor[0][1] + full[0][2] * cofactor[0][2]
    clamped = jnp.maximum(volume, 0.3)
    mu, weight = shear[...], weights[...]
    factor = (bulk[...] * jnp.log(clamped) - mu) / clamped
    for i in range(3):
        for j in range(3):
            field[j, pl.ds(i, 32, stride=4), :] = weight * (mu * full[i][j] + factor * cofactor[i][j])
    low_lane = lax.broadcasted_iota(jnp.int32, (1, 384), 1) < 192
    rows_pair = lax.broadcasted_iota(jnp.int32, (128, 384), 0)

    def forces(quad, carry):
        for pair in range(2):
            total = None
            for j in range(3):
                first = 4 * quad + 2 * pair
                at = pl.ds(pl.multiple_of(16 * quad + 8 * pair, 8), 8)
                both = jnp.concatenate([grads[first, j], grads[first + 1, j]], axis=0)
                part = lax.dot_general(field[j, at, :].astype(BF), both, NT, preferred_element_type=F32)
                total = part if total is None else total + part
            span = slice(384 * pair, 384 * pair + 384)
            mask = rows_pair == ((nodes[quad, :, span] >> 8) & 127)
            for i in range(3):
                value = jnp.where(low_lane, total[i : i + 1], total[4 + i : 5 + i])
                spread[quad, 128 * i : 128 * i + 128, span] = jnp.where(mask, value, 0.0).astype(BF)
        return carry

    lax.fori_loop(0, 8, forces, 0)
    for side in range(3):
        total = None
        for quad in range(8):
            part = lax.dot_general(spread[quad], columns[quad, side], NT, preferred_element_type=F32)
            total = part if total is None else total + part
        for i in range(3):
            out[side, i] = total[128 * i : 128 * i + 128].astype(BF)


def cells(nodes, table, weights, shear, bulk, grads):
    vmem = pl.BlockSpec(memory_space=pltpu.VMEM)
    return pl.pallas_call(
        cells_kernel,
        name="cells",
        out_shape=jax.ShapeDtypeStruct((3, 3, 128, 256), BF),
        in_specs=[vmem] * 5 + [pl.BlockSpec(memory_space=pl.ANY)],
        out_specs=vmem,
        scratch_shapes=[
            pltpu.VMEM((32, 3, 192, 128), BF),
            pltpu.VMEM((3, 128, 128), F32),
            pltpu.VMEM((8, 8, QUAD), F32),
            pltpu.VMEM((8, 3, 256, QUAD), BF),
            pltpu.VMEM((8, 384, QUAD), BF),
            pltpu.SemaphoreType.DMA,
        ],
        compiler_params=pltpu.CompilerParams(vmem_limit_bytes=56 << 20),
    )(nodes, table, weights, shear, bulk, grads)


def finish_kernel(
    forces, now, prev, inv_mass, owner, block_nodes, phi_hbm, corr_hbm, target, fixed, out,
    got, summed, state, asking, asked, answer, answered, giving, given, adding, part, halves,
    phi, corr, phi_bf, corr_bf, goal, held, numbers, values, deltas, permuted, gathered,
    load_sem, force_send, force_recv, all_send, all_recv, ask_send, ask_recv, ans_send, ans_recv,
    give_send, give_recv, part_send, part_recv, half_send, half_recv,
):
    slab, group = lax.axis_index("slab"), lax.axis_index("group")
    slabs, groups = 16, 8

    def slab_at(by):
        return lax.rem(slab + by + slabs, slabs)

    def group_at(by):
        return lax.rem(group + by + groups, groups)

    barrier = pltpu.get_barrier_semaphore()

    def near_of(k):
        step = k + 1
        return step // groups, lax.rem(step, groups)

    def near_device(k):
        side, step = near_of(k)
        shift = jnp.where(side == 0, 0, jnp.where(side == 1, 1, -1))
        return slab_at(shift), group_at(step)

    def greet(k, carry):
        pl.semaphore_signal(barrier, inc=1, device_id=near_device(k), device_id_type=MESH)
        return carry

    def greet_far(k, carry):
        pl.semaphore_signal(barrier, inc=1, device_id=(slab_at(k), group), device_id_type=MESH)
        return carry

    lax.fori_loop(0, 23, greet, 0)
    lax.fori_loop(2, 15, greet_far, 0)
    load_phi = pltpu.make_async_copy(phi_hbm, phi, load_sem.at[0])
    load_corr = pltpu.make_async_copy(corr_hbm, corr, load_sem.at[1])
    load_own = pltpu.make_async_copy(
        forces.at[1, :, pl.ds(pl.multiple_of(group * 16, 16), 16), :], got.at[23], load_sem.at[2]
    )
    load_phi.start()
    load_corr.start()
    load_own.start()
    pl.semaphore_wait(barrier, 36)

    def force_copy(k):
        side, step = near_of(k)
        source = jnp.where(side == 0, 1, jnp.where(side == 1, 2, 0))
        start = pl.multiple_of(group_at(step) * 16, 16)
        return pltpu.make_async_remote_copy(
            src_ref=forces.at[source, :, pl.ds(start, 16), :],
            dst_ref=got.at[k],
            send_sem=force_send.at[k],
            recv_sem=force_recv.at[k],
            device_id=near_device(k),
            device_id_type=MESH,
        )

    def start_force(k, carry):
        force_copy(k).start()
        return carry

    lax.fori_loop(0, 23, start_force, 0)

    own_row = owner[...]
    diag = lax.broadcasted_iota(jnp.int32, (32, 32), 0) == lax.broadcasted_iota(jnp.int32, (32, 32), 1)
    own_col = jnp.sum(jnp.where(diag, own_row, 0), axis=1, keepdims=True)
    block_wide = lax.broadcasted_iota(jnp.int32, (32, 128), 0)
    of_lane = lax.broadcasted_iota(jnp.int32, (32, 128), 1) // 4
    own_wide = jnp.sum(jnp.where(block_wide == of_lane, own_col, 0), axis=0, keepdims=True)
    earlier = (own_col == own_wide) & (block_wide < of_lane)
    rank = jnp.sum(jnp.where(earlier, 1, 0), axis=0, keepdims=True)
    relative = own_wide - slab
    relative = jnp.where(relative < 0, relative + slabs, relative)
    key = relative * 16 + rank * 4 + lax.broadcasted_iota(jnp.int32, (1, 128), 1) % 4
    to_slots = onehot(key, 256)
    square = lax.broadcasted_iota(jnp.int32, (128, 128), 0) == lax.broadcasted_iota(jnp.int32, (128, 128), 1)
    key_col = jnp.sum(jnp.where(square, key, 0), axis=1, keepdims=True)
    to_blocks = jnp.where(lax.broadcasted_iota(jnp.int32, (128, 256), 1) == key_col, 1.0, 0.0).astype(BF)

    node = block_nodes[...]
    numbers[...] = jnp.zeros_like(numbers)
    for side in range(2):
        span = slice(128 * side, 128 * side + 128)
        numbers[side, pl.ds(0, 32, stride=4), :] = ((node[:, span] >> 8) + 1).astype(F32)
        numbers[side, pl.ds(1, 32, stride=4), :] = ((node[:, span] & 255) + 1).astype(F32)
    named = jnp.concatenate([numbers[0], numbers[1]], axis=1).astype(BF)
    asks = jnp.dot(to_slots, named, preferred_element_type=F32) - 1.0
    for q in range(16):
        asking[q] = asks[16 * q : 16 * q + 16].astype(BF)

    def exchange(source, landing, send, recv):
        def copy(q):
            return pltpu.make_async_remote_copy(
                src_ref=source.at[q],
                dst_ref=landing.at[slabs - q],
                send_sem=send.at[q],
                recv_sem=recv.at[slabs - q],
                device_id=(slab_at(q), group),
                device_id_type=MESH,
            )

        def arrival(q):
            return pltpu.make_async_remote_copy(
                src_ref=source.at[q],
                dst_ref=landing.at[q],
                send_sem=send.at[q],
                recv_sem=recv.at[q],
                device_id=(slab_at(q), group),
                device_id_type=MESH,
            )

        return copy, arrival

    ask_copy, ask_arrival = exchange(asking, asked, ask_send, ask_recv)
    ans_copy, ans_arrival = exchange(answer, answered, ans_send, ans_recv)
    give_copy, give_arrival = exchange(giving, given, give_send, give_recv)

    def start_ask(q, carry):
        ask_copy(q).start()
        return carry

    lax.fori_loop(1, 16, start_ask, 0)
    asked[0] = asking[0]
    for i in range(3):
        goal[pl.ds(i, 32, stride=4), :] = target[i]
    goal[pl.ds(3, 32, stride=4), :] = jnp.zeros((32, 128), F32)
    for i in range(4):
        held[pl.ds(i, 32, stride=4), :] = fixed[...].astype(F32)
    load_phi.wait()
    load_corr.wait()

    def narrow(pair, carry):
        phi_bf[pair] = phi[pair].astype(BF)
        corr_bf[pair] = corr[pair].astype(BF)
        return carry

    lax.fori_loop(0, 16, narrow, 0)
    load_own.wait()

    share = got[23].astype(F32)
    for k in range(23):
        force_copy(k).wait_recv()
        side = (k + 1) // groups
        piece = got[k].astype(F32)
        if side == 1:
            piece = jnp.where(slab == 0, 0.0, piece)
        if side == 2:
            piece = jnp.where(slab == slabs - 1, 0.0, piece)
        share = share + piece

    mine = pl.ds(pl.multiple_of(group * 16, 16), 16)

    def shared(buffer, send, recv):
        def copy(step):
            return pltpu.make_async_remote_copy(
                src_ref=buffer.at[:, mine, :],
                dst_ref=buffer.at[:, mine, :],
                send_sem=send.at[step],
                recv_sem=recv.at[groups - step],
                device_id=(slab, group_at(step)),
                device_id_type=MESH,
            )

        def arrival(step):
            theirs = pl.ds(pl.multiple_of(group_at(step) * 16, 16), 16)
            return pltpu.make_async_remote_copy(
                src_ref=buffer.at[:, theirs, :],
                dst_ref=buffer.at[:, theirs, :],
                send_sem=send.at[step],
                recv_sem=recv.at[step],
                device_id=(slab, group_at(step)),
                device_id_type=MESH,
            )

        return copy, arrival

    sum_copy, sum_arrival = shared(summed, all_send, all_recv)
    half_copy, half_arrival = shared(halves, half_send, half_recv)
    summed[:, mine, :] = share.astype(BF)
    for step in range(1, groups):
        sum_copy(step).start()
    for i in range(3):
        state[i] = 2.0 * now[i] - prev[i]
    for step in range(1, groups):
        sum_arrival(step).wait_recv()
    for i in range(3):
        state[i] = state[i] - inv_mass[...] * summed[i].astype(F32)
        gathered[128 * i : 128 * i + 128, :] = state[i].astype(BF)

    rows_of = lax.broadcasted_iota(jnp.int32, (128, 1024), 0)
    sixteen = lax.broadcasted_iota(jnp.int32, (16, 256), 0)

    def spots(q):
        spot = asked[q].astype(F32)
        row = jnp.concatenate([spot[4 * c : 4 * c + 1] for c in range(CAP)], axis=1).astype(jnp.int32)
        column = jnp.concatenate([spot[4 * c + 1 : 4 * c + 2] for c in range(CAP)], axis=1).astype(jnp.int32)
        return row, column

    def look(q):
        row, column = spots(q)
        hit = jnp.dot(gathered[...], onehot(column, 256), preferred_element_type=F32)
        mask = rows_of == row
        found = jnp.zeros((16, 256), F32)
        for i in range(3):
            line = jnp.sum(jnp.where(mask, hit[128 * i : 128 * i + 128], 0.0), axis=0, keepdims=True)
            for c in range(CAP):
                found = jnp.where(sixteen == 4 * c + i, line[:, 256 * c : 256 * c + 256], found)
        answer[q] = found.astype(BF)

    def look_far(q, carry):
        ask_arrival(q).wait_recv()
        look(q)
        ans_copy(q).start()
        return carry

    lax.fori_loop(1, 16, look_far, 0)
    look(0)
    permuted[0:16] = answer[0]

    def take(q, carry):
        ans_arrival(q).wait_recv()
        permuted[pl.ds(pl.multiple_of(q * 16, 16), 16), :] = answered[q]
        return carry

    lax.fori_loop(1, 16, take, 0)
    values[...] = jnp.dot(to_blocks, permuted[...], preferred_element_type=F32)

    upper = lax.broadcasted_iota(jnp.int32, (8, 128), 0) < 4

    def correct(pair, carry):
        at = pl.ds(pl.multiple_of(8 * pair, 8), 8)
        both = lax.dot_general(values[at, :].astype(BF), phi_bf[pair], NT, preferred_element_type=F32)
        interp = jnp.where(upper, both[:, :128], both[:, 128:])
        resid = held[at, :] * (goal[at, :] - interp)
        both = lax.dot_general(resid.astype(BF), corr_bf[pair], NT, preferred_element_type=F32)
        wide = jnp.concatenate([jnp.where(upper, both[:, :128], 0.0), jnp.where(upper, 0.0, both[:, 128:])], axis=1)
        deltas[at, :] = jnp.dot(wide.astype(BF), phi_bf[pair], preferred_element_type=F32)
        return carry

    lax.fori_loop(0, 16, correct, 0)
    gives = jnp.dot(to_slots, deltas[...].astype(BF), preferred_element_type=F32).astype(BF)
    for q in range(16):
        giving[q] = gives[16 * q : 16 * q + 16]

    def start_give(q, carry):
        give_copy(q).start()
        return carry

    lax.fori_loop(1, 16, start_give, 0)
    given[0] = giving[0]

    def place(q):
        row, column = spots(q)
        mask = rows_of == row
        amount = given[q].astype(F32)
        lines = []
        for i in range(3):
            line = jnp.concatenate([amount[4 * c + i : 4 * c + i + 1] for c in range(CAP)], axis=1)
            lines.append(jnp.where(mask, line, 0.0).astype(BF))
        return lax.dot_general(
            jnp.concatenate(lines, axis=0), onehot(column, 256), NT, preferred_element_type=F32
        )

    adding[...] = place(0)

    def place_far(q, carry):
        give_arrival(q).wait_recv()
        adding[...] += place(q)
        return carry

    lax.fori_loop(1, 16, place_far, 0)
    for i in range(3):
        part[0, i] = adding[128 * i : 128 * i + 128, :].astype(BF)

    def part_copy(step):
        theirs = pl.ds(pl.multiple_of(group_at(step) * 16, 16), 16)
        return pltpu.make_async_remote_copy(
            src_ref=part.at[0, :, theirs, :],
            dst_ref=got.at[24 + groups - step],
            send_sem=part_send.at[step],
            recv_sem=part_recv.at[groups - step],
            device_id=(slab, group_at(step)),
            device_id_type=MESH,
        )

    def part_arrival(step):
        theirs = pl.ds(pl.multiple_of(group_at(step) * 16, 16), 16)
        return pltpu.make_async_remote_copy(
            src_ref=part.at[0, :, theirs, :],
            dst_ref=got.at[24 + step],
            send_sem=part_send.at[step],
            recv_sem=part_recv.at[step],
            device_id=(slab, group_at(step)),
            device_id_type=MESH,
        )

    for step in range(1, groups):
        part_copy(step).start()
    share = jnp.stack([adding[pl.ds(pl.multiple_of(128 * i + group * 16, 16), 16), :] for i in range(3)])
    for step in range(1, groups):
        part_arrival(step).wait_recv()
        share = share + got[24 + step].astype(F32)
    halves[:, mine, :] = share.astype(BF)
    for step in range(1, groups):
        half_copy(step).start()
    for step in range(1, groups):
        half_arrival(step).wait_recv()
    for i in range(3):
        out[i] = state[i] + halves[i].astype(F32)

    def end_force(k, carry):
        force_copy(k).wait_send()
        return carry

    def end_far(q, carry):
        ask_copy(q).wait_send()
        ans_copy(q).wait_send()
        give_copy(q).wait_send()
        return carry

    def end_near(step, carry):
        sum_copy(step).wait_send()
        part_copy(step).wait_send()
        half_copy(step).wait_send()
        return carry

    lax.fori_loop(0, 23, end_force, 0)
    lax.fori_loop(1, 16, end_far, 0)
    lax.fori_loop(1, groups, end_near, 0)


def finish(forces, now, prev, inv_mass, owner, block_nodes, phi, corr, target, fixed):
    vmem = pl.BlockSpec(memory_space=pltpu.VMEM)
    anywhere = pl.BlockSpec(memory_space=pl.ANY)
    dma = pltpu.SemaphoreType.DMA
    message = pltpu.VMEM((16, 16, 256), BF)
    nodal = pltpu.VMEM((3, 128, 256), BF)
    return pl.pallas_call(
        finish_kernel,
        name="finish",
        out_shape=jax.ShapeDtypeStruct((3, 128, 256), F32),
        in_specs=[anywhere] + [vmem] * 5 + [anywhere] * 2 + [vmem] * 2,
        out_specs=vmem,
        scratch_shapes=[
            pltpu.VMEM((32, 3, 16, 256), BF),
            nodal,
            pltpu.VMEM((3, 128, 256), F32),
            message, message, message, message, message, message,
            pltpu.VMEM((384, 256), F32),
            pltpu.VMEM((1, 3, 128, 256), BF),
            nodal,
            pltpu.VMEM((16, 256, 256), F32),
            pltpu.VMEM((16, 256, 128), F32),
            pltpu.VMEM((16, 256, 256), BF),
            pltpu.VMEM((16, 256, 128), BF),
            pltpu.VMEM((128, 128), F32),
            pltpu.VMEM((128, 128), F32),
            pltpu.VMEM((2, 128, 128), F32),
            pltpu.VMEM((128, 256), F32),
            pltpu.VMEM((128, 256), F32),
            pltpu.VMEM((256, 256), BF),
            pltpu.VMEM((384, 256), BF),
            dma((3,)), dma((23,)), dma((23,)), dma((8,)), dma((8,)), dma((16,)), dma((16,)), dma((16,)), dma((16,)),
            dma((16,)), dma((16,)), dma((8,)), dma((8,)), dma((8,)), dma((8,)),
        ],
        compiler_params=pltpu.CompilerParams(
            vmem_limit_bytes=48 << 20, collective_id=0, has_side_effects=True
        ),
    )(forces, now, prev, inv_mass, owner, block_nodes, phi, corr, target, fixed)


def body(
    disp_now, disp_prev, inv_mass, cell_nodes, shape_grads, cell_weights, cell_shear, cell_bulk,
    block_owner, block_nodes, block_phi, block_corr, block_target, block_fixed,
):
    own = disp_now.astype(BF).reshape(384, 256)
    count = lax.axis_size("slab")
    forward = [(i, i + 1) for i in range(count - 1)]
    backward = [(b, a) for a, b in forward]
    low = lax.ppermute(own, "slab", forward)
    high = lax.ppermute(own, "slab", backward)
    table = jnp.stack([low, own, high])
    forces = cells(
        cell_nodes.reshape(8, 1, QUAD), table, cell_weights, cell_shear[:, None], cell_bulk[:, None], shape_grads
    )
    result = finish(
        forces,
        disp_now.reshape(3, 128, 256),
        disp_prev.reshape(3, 128, 256),
        inv_mass.reshape(128, 256),
        block_owner.reshape(1, 32),
        block_nodes,
        block_phi.reshape(16, 256, 256),
        block_corr.reshape(16, 256, 128),
        jnp.moveaxis(block_target, 1, 0),
        block_fixed,
    )
    return result.reshape(3, 32768)


def solution(mesh):
    both = ("slab", "group")
    placed = (
        P(None, "slab"), P(None, "slab"), P("slab"), P(both, None), P(both, None, None, None), P(both, None),
        P(both), P(both), P(both, None), P(both, None), P(both, None, None), P(both, None, None),
        P(both, None, None), P(both, None),
    )
    return jax.shard_map(body, mesh=mesh, in_specs=placed, out_specs=P(None, "slab"), check_vma=False)
```

```python
import jax
import jax.numpy as jnp
from jax import lax
from jax.experimental import pallas as pl
from jax.experimental.pallas import tpu as pltpu
from jax.sharding import PartitionSpec as P

BF = jnp.bfloat16
F32 = jnp.float32
NT = (((1,), (1,)), ((), ()))
MESH = pl.DeviceIdType.MESH
CAP = 4
QUAD = 768


def onehot(index, size):
    rows = lax.broadcasted_iota(jnp.int32, (size, index.shape[1]), 0)
    return jnp.where(rows == index, 1.0, 0.0).astype(BF)


def step_kernel(
    now_hbm, prev_hbm, mass_hbm, cell_nodes, grads_hbm, weights, shear, bulk, owner, block_nodes, phi_hbm, corr_hbm,
    target, fixed, out,
    lines, prev, mass, state, tables, nodes, grads, field, near, columns, spread, forces,
    got, summed, asking, asked, answer, answered, giving, given, adding, part, halves,
    phi, corr, phi_bf, corr_bf, goal, held, numbers, values, resids, permuted, gathered, hots,
    load_sem, halo_send, halo_recv, force_send, force_recv, all_send, all_recv, ask_send, ask_recv, ans_send, ans_recv,
    give_send, give_recv, part_send, part_recv, half_send, half_recv,
):
    slab, group = lax.axis_index("slab"), lax.axis_index("group")
    slabs, groups = 16, 8

    def slab_at(by):
        return lax.rem(slab + by + slabs, slabs)

    def group_at(by):
        return lax.rem(group + by + groups, groups)

    load_now = pltpu.make_async_copy(now_hbm, lines, load_sem.at[0])
    load_grads = pltpu.make_async_copy(grads_hbm, grads, load_sem.at[1])
    load_prev = pltpu.make_async_copy(prev_hbm, prev, load_sem.at[2])
    load_mass = pltpu.make_async_copy(mass_hbm, mass, load_sem.at[3])
    load_phi = pltpu.make_async_copy(phi_hbm, phi, load_sem.at[4])
    load_corr = pltpu.make_async_copy(corr_hbm, corr, load_sem.at[5])
    load_now.start()
    load_grads.start()
    load_prev.start()
    load_mass.start()
    load_phi.start()
    load_corr.start()

    barrier = pltpu.get_barrier_semaphore()

    def near_device(k):
        shift = jnp.where(k < 8, -1, jnp.where(k < 16, 1, 0))
        return slab_at(shift), group_at(lax.rem(k + 1, groups))

    def greet(k, carry):
        pl.semaphore_signal(barrier, inc=1, device_id=near_device(k), device_id_type=MESH)
        return carry

    def greet_far(k, carry):
        pl.semaphore_signal(barrier, inc=1, device_id=(slab_at(k), group), device_id_type=MESH)
        return carry

    lax.fori_loop(0, 23, greet, 0)
    lax.fori_loop(2, 15, greet_far, 0)

    def relaid(source, use):
        def move(block, carry):
            start = pl.multiple_of(block * 2048, 2048)
            wide = source[:, pl.ds(start, 2048)]
            at = pl.ds(pl.multiple_of(block * 8, 8), 8)
            for i in range(3):
                use(i, at, jnp.concatenate([wide[i : i + 1, 256 * r : 256 * r + 256] for r in range(8)], axis=0))
            return carry

        lax.fori_loop(0, 16, move, 0)

    def set_state(i, at, value):
        state[i, at, :] = value

    load_now.wait()
    relaid(lines, set_state)
    for i in range(3):
        tables[1, 128 * i : 128 * i + 128, :] = state[i].astype(BF)
    pl.semaphore_wait(barrier, 36)

    def halo(side, by):
        return pltpu.make_async_remote_copy(
            src_ref=tables.at[1],
            dst_ref=tables.at[side],
            send_sem=halo_send.at[side],
            recv_sem=halo_recv.at[side],
            device_id=(slab_at(by), group),
            device_id_type=MESH,
        )

    to_above, to_below = halo(0, 1), halo(2, -1)
    to_above.start()
    to_below.start()

    own_row = owner[...]
    diag = lax.broadcasted_iota(jnp.int32, (32, 32), 0) == lax.broadcasted_iota(jnp.int32, (32, 32), 1)
    own_col = jnp.sum(jnp.where(diag, own_row, 0), axis=1, keepdims=True)
    block_wide = lax.broadcasted_iota(jnp.int32, (32, 128), 0)
    of_lane = lax.broadcasted_iota(jnp.int32, (32, 128), 1) // 4
    own_wide = jnp.sum(jnp.where(block_wide == of_lane, own_col, 0), axis=0, keepdims=True)
    earlier = (own_col == own_wide) & (block_wide < of_lane)
    rank = jnp.sum(jnp.where(earlier, 1, 0), axis=0, keepdims=True)
    relative = own_wide - slab
    relative = jnp.where(relative < 0, relative + slabs, relative)
    key = relative * 16 + rank * 4 + lax.broadcasted_iota(jnp.int32, (1, 128), 1) % 4
    to_slots = onehot(key, 256)
    square = lax.broadcasted_iota(jnp.int32, (128, 128), 0) == lax.broadcasted_iota(jnp.int32, (128, 128), 1)
    key_col = jnp.sum(jnp.where(square, key, 0), axis=1, keepdims=True)

    node = block_nodes[...]
    numbers[...] = jnp.zeros_like(numbers)
    for side in range(2):
        span = slice(128 * side, 128 * side + 128)
        numbers[side, pl.ds(0, 32, stride=4), :] = ((node[:, span] >> 8) + 1).astype(F32)
        numbers[side, pl.ds(1, 32, stride=4), :] = ((node[:, span] & 255) + 1).astype(F32)
    named = jnp.concatenate([numbers[0], numbers[1]], axis=1).astype(BF)
    asks = jnp.dot(to_slots, named, preferred_element_type=F32) - 1.0
    for q in range(16):
        asking[q] = asks[16 * q : 16 * q + 16].astype(BF)

    def exchange(source, landing, send, recv):
        def copy(q):
            return pltpu.make_async_remote_copy(
                src_ref=source.at[q],
                dst_ref=landing.at[slabs - q],
                send_sem=send.at[q],
                recv_sem=recv.at[slabs - q],
                device_id=(slab_at(q), group),
                device_id_type=MESH,
            )

        def arrival(q):
            return pltpu.make_async_remote_copy(
                src_ref=source.at[q],
                dst_ref=landing.at[q],
                send_sem=send.at[q],
                recv_sem=recv.at[q],
                device_id=(slab_at(q), group),
                device_id_type=MESH,
            )

        return copy, arrival

    ask_copy, ask_arrival = exchange(asking, asked, ask_send, ask_recv)
    ans_copy, ans_arrival = exchange(answer, answered, ans_send, ans_recv)
    give_copy, give_arrival = exchange(giving, given, give_send, give_recv)

    def start_ask(q, carry):
        ask_copy(q).start()
        return carry

    lax.fori_loop(1, 16, start_ask, 0)
    asked[0] = asking[0]

    def flatten(quad, carry):
        rows = [cell_nodes[pl.ds(4 * quad + e, 1), :] for e in range(4)]
        nodes[quad] = jnp.concatenate(rows, axis=1)
        return carry

    lax.fori_loop(0, 8, flatten, 0)
    rows_quad = lax.broadcasted_iota(jnp.int32, (128, QUAD), 0)

    def pick(total, row):
        mask = rows_quad == row
        return [
            jnp.sum(jnp.where(mask, total[128 * i : 128 * i + 128], 0.0), axis=0, keepdims=True) for i in range(3)
        ]

    def gather_own(quad, carry):
        number = nodes[quad]
        side_of, row, column = number >> 15, (number >> 8) & 127, number & 255
        for side in range(3):
            columns[quad, side] = onehot(jnp.where(side_of == side, column, -1), 256)
        total = jnp.dot(tables[1], columns[quad, 1], preferred_element_type=F32)
        for i, line in enumerate(pick(total, row)):
            near[quad, i : i + 1, :] = line
        return carry

    lax.fori_loop(0, 8, gather_own, 0)
    to_above.wait_recv()
    to_below.wait_recv()
    tables[0] = jnp.where(slab == 0, 0.0, tables[0].astype(F32)).astype(BF)
    tables[2] = jnp.where(slab == slabs - 1, 0.0, tables[2].astype(F32)).astype(BF)

    def gather_sides(quad, carry):
        row = (nodes[quad] >> 8) & 127
        total = jnp.dot(tables[0], columns[quad, 0], preferred_element_type=F32)
        total += jnp.dot(tables[2], columns[quad, 2], preferred_element_type=F32)
        for i, line in enumerate(pick(total, row)):
            near[quad, i : i + 1, :] += line
        return carry

    lax.fori_loop(0, 8, gather_sides, 0)
    load_grads.wait()
    sub = lax.broadcasted_iota(jnp.int32, (8, 384), 0)
    lane = lax.broadcasted_iota(jnp.int32, (8, 384), 1)
    own = (sub >= 4) == (lane >= 192)

    def gradient(quad, carry):
        for pair in range(2):
            left = jnp.zeros((8, 384), F32)
            for i in range(3):
                left = jnp.where(sub % 4 == i, near[quad, i : i + 1, 384 * pair : 384 * pair + 384], left)
            left = jnp.where(own, left, 0.0).astype(BF)
            for j in range(3):
                first = 4 * quad + 2 * pair
                both = jnp.concatenate([grads[first, j], grads[first + 1, j]], axis=0)
                at = pl.ds(pl.multiple_of(16 * quad + 8 * pair, 8), 8)
                field[j, at, :] = jnp.dot(left, both, preferred_element_type=F32)
        return carry

    lax.fori_loop(0, 8, gradient, 0)
    full = [
        [field[j, pl.ds(i, 32, stride=4), :] + (1.0 if i == j else 0.0) for j in range(3)]
        for i in range(3)
    ]
    cofactor = [
        [
            full[(i + 1) % 3][(j + 1) % 3] * full[(i + 2) % 3][(j + 2) % 3]
            - full[(i + 1) % 3][(j + 2) % 3] * full[(i + 2) % 3][(j + 1) % 3]
            for j in range(3)
        ]
        for i in range(3)
    ]
    volume = full[0][0] * cofactor[0][0] + full[0][1] * cofactor[0][1] + full[0][2] * cofactor[0][2]
    clamped = jnp.maximum(volume, 0.3)
    mu = jnp.sum(jnp.where(diag, shear[...], 0.0), axis=1, keepdims=True)
    lam = jnp.sum(jnp.where(diag, bulk[...], 0.0), axis=1, keepdims=True)
    weight = weights[...]
    factor = (lam * jnp.log(clamped) - mu) / clamped
    for i in range(3):
        for j in range(3):
            field[j, pl.ds(i, 32, stride=4), :] = weight * (mu * full[i][j] + factor * cofactor[i][j])
    low_lane = lax.broadcasted_iota(jnp.int32, (1, 384), 1) < 192
    rows_pair = lax.broadcasted_iota(jnp.int32, (128, 384), 0)

    def cell_forces(quad, carry):
        for pair in range(2):
            total = None
            for j in range(3):
                first = 4 * quad + 2 * pair
                at = pl.ds(pl.multiple_of(16 * quad + 8 * pair, 8), 8)
                both = jnp.concatenate([grads[first, j], grads[first + 1, j]], axis=0)
                piece = lax.dot_general(field[j, at, :].astype(BF), both, NT, preferred_element_type=F32)
                total = piece if total is None else total + piece
            span = slice(384 * pair, 384 * pair + 384)
            mask = rows_pair == ((nodes[quad, :, span] >> 8) & 127)
            for i in range(3):
                value = jnp.where(low_lane, total[i : i + 1], total[4 + i : 5 + i])
                spread[quad, 128 * i : 128 * i + 128, span] = jnp.where(mask, value, 0.0).astype(BF)
        return carry

    lax.fori_loop(0, 8, cell_forces, 0)

    def force_copy(k):
        source = jnp.where(k < 8, 0, jnp.where(k < 16, 2, 1))
        start = pl.multiple_of(group_at(lax.rem(k + 1, groups)) * 16, 16)
        return pltpu.make_async_remote_copy(
            src_ref=forces.at[source, :, pl.ds(start, 16), :],
            dst_ref=got.at[k],
            send_sem=force_send.at[k],
            recv_sem=force_recv.at[k],
            device_id=near_device(k),
            device_id_type=MESH,
        )

    def start_force(k, carry):
        force_copy(k).start()
        return carry

    for side, first, last in ((0, 0, 8), (2, 8, 16), (1, 16, 23)):
        total = None
        for quad in range(8):
            piece = lax.dot_general(spread[quad], columns[quad, side], NT, preferred_element_type=F32)
            total = piece if total is None else total + piece
        for i in range(3):
            forces[side, i] = total[128 * i : 128 * i + 128].astype(BF)
        lax.fori_loop(first, last, start_force, 0)

    load_prev.wait()

    def set_base(i, at, value):
        state[i, at, :] = 2.0 * state[i, at, :] - value

    relaid(prev, set_base)

    def spots(q):
        spot = asked[q].astype(F32)
        row = jnp.concatenate([spot[4 * c : 4 * c + 1] for c in range(CAP)], axis=1).astype(jnp.int32)
        column = jnp.concatenate([spot[4 * c + 1 : 4 * c + 2] for c in range(CAP)], axis=1).astype(jnp.int32)
        return row, column

    def heat(q):
        hots[q] = onehot(spots(q)[1], 256)

    def heat_far(q, carry):
        ask_arrival(q).wait_recv()
        heat(q)
        return carry

    heat(0)
    lax.fori_loop(1, 16, heat_far, 0)
    for i in range(3):
        goal[pl.ds(i, 32, stride=4), :] = target[i]
    goal[pl.ds(3, 32, stride=4), :] = jnp.zeros((32, 128), F32)
    for i in range(4):
        held[pl.ds(i, 32, stride=4), :] = fixed[...].astype(F32)
    load_phi.wait()
    load_corr.wait()

    def narrow(pair, carry):
        phi_bf[pair] = phi[pair].astype(BF)
        corr_bf[pair] = corr[pair].astype(BF)
        return carry

    lax.fori_loop(0, 16, narrow, 0)
    load_mass.wait()

    mine = pl.ds(pl.multiple_of(group * 16, 16), 16)
    share = forces[1, :, mine, :].astype(F32)
    for k in range(23):
        force_copy(k).wait_recv()
        piece = got[k].astype(F32)
        if k < 8:
            piece = jnp.where(slab == slabs - 1, 0.0, piece)
        elif k < 16:
            piece = jnp.where(slab == 0, 0.0, piece)
        share = share + piece

    def shared(buffer, send, recv):
        def copy(step):
            return pltpu.make_async_remote_copy(
                src_ref=buffer.at[:, mine, :],
                dst_ref=buffer.at[:, mine, :],
                send_sem=send.at[step],
                recv_sem=recv.at[groups - step],
                device_id=(slab, group_at(step)),
                device_id_type=MESH,
            )

        def arrival(step):
            theirs = pl.ds(pl.multiple_of(group_at(step) * 16, 16), 16)
            return pltpu.make_async_remote_copy(
                src_ref=buffer.at[:, theirs, :],
                dst_ref=buffer.at[:, theirs, :],
                send_sem=send.at[step],
                recv_sem=recv.at[step],
                device_id=(slab, group_at(step)),
                device_id_type=MESH,
            )

        return copy, arrival

    sum_copy, sum_arrival = shared(summed, all_send, all_recv)
    half_copy, half_arrival = shared(halves, half_send, half_recv)
    summed[:, mine, :] = share.astype(BF)
    for step in range(1, groups):
        sum_copy(step).start()
    scale = jnp.concatenate([mass[pl.ds(0, 128, stride=2), :], mass[pl.ds(1, 128, stride=2), :]], axis=1)
    for step in range(1, groups):
        sum_arrival(step).wait_recv()
    for i in range(3):
        state[i] = state[i] - scale * summed[i].astype(F32)
        gathered[128 * i : 128 * i + 128, :] = state[i].astype(BF)

    rows_of = lax.broadcasted_iota(jnp.int32, (128, 1024), 0)
    sixteen = lax.broadcasted_iota(jnp.int32, (16, 256), 0)

    def look(q):
        row, _ = spots(q)
        hit = jnp.dot(gathered[...], hots[q], preferred_element_type=F32)
        mask = rows_of == row
        found = jnp.zeros((16, 256), F32)
        for i in range(3):
            line = jnp.sum(jnp.where(mask, hit[128 * i : 128 * i + 128], 0.0), axis=0, keepdims=True)
            for c in range(CAP):
                found = jnp.where(sixteen == 4 * c + i, line[:, 256 * c : 256 * c + 256], found)
        answer[q] = found.astype(BF)

    def look_far(q, carry):
        look(q)
        ans_copy(q).start()
        return carry

    lax.fori_loop(1, 16, look_far, 0)
    look(0)
    permuted[0:16] = answer[0]
    to_blocks = jnp.where(lax.broadcasted_iota(jnp.int32, (128, 256), 1) == key_col, 1.0, 0.0).astype(BF)

    def take(q, carry):
        ans_arrival(q).wait_recv()
        permuted[pl.ds(pl.multiple_of(q * 16, 16), 16), :] = answered[q]
        return carry

    lax.fori_loop(1, 16, take, 0)
    values[...] = jnp.dot(to_blocks, permuted[...], preferred_element_type=F32)

    upper = lax.broadcasted_iota(jnp.int32, (8, 128), 0) < 4

    def at_pair(pair):
        return pl.ds(pl.multiple_of(8 * pair, 8), 8)

    def residual(pair, carry):
        at = at_pair(pair)
        both = lax.dot_general(values[at, :].astype(BF), phi_bf[pair], NT, preferred_element_type=F32)
        interp = jnp.where(upper, both[:, :128], both[:, 128:])
        resids[at, :] = held[at, :] * (goal[at, :] - interp)
        return carry

    def correction(pair, carry):
        at = at_pair(pair)
        both = lax.dot_general(resids[at, :].astype(BF), corr_bf[pair], NT, preferred_element_type=F32)
        values[at, 0:128] = jnp.where(upper, both[:, :128], 0.0)
        values[at, 128:256] = jnp.where(upper, 0.0, both[:, 128:])
        return carry

    def spreading(pair, carry):
        at = at_pair(pair)
        values[at, :] = jnp.dot(values[at, :].astype(BF), phi_bf[pair], preferred_element_type=F32)
        return carry

    lax.fori_loop(0, 16, residual, 0, unroll=8)
    lax.fori_loop(0, 16, correction, 0, unroll=8)
    lax.fori_loop(0, 16, spreading, 0, unroll=8)
    gives = jnp.dot(to_slots, values[...].astype(BF), preferred_element_type=F32).astype(BF)
    for q in range(16):
        giving[q] = gives[16 * q : 16 * q + 16]

    def start_give(q, carry):
        give_copy(q).start()
        return carry

    lax.fori_loop(1, 16, start_give, 0)
    given[0] = giving[0]

    def place(q):
        row, _ = spots(q)
        mask = rows_of == row
        amount = given[q].astype(F32)
        rows = []
        for i in range(3):
            line = jnp.concatenate([amount[4 * c + i : 4 * c + i + 1] for c in range(CAP)], axis=1)
            rows.append(jnp.where(mask, line, 0.0).astype(BF))
        return lax.dot_general(jnp.concatenate(rows, axis=0), hots[q], NT, preferred_element_type=F32)

    adding[...] = place(0)

    def place_far(q, carry):
        give_arrival(q).wait_recv()
        adding[...] += place(q)
        return carry

    lax.fori_loop(1, 16, place_far, 0)
    for i in range(3):
        part[i] = adding[128 * i : 128 * i + 128, :].astype(BF)

    def part_copy(step):
        theirs = pl.ds(pl.multiple_of(group_at(step) * 16, 16), 16)
        return pltpu.make_async_remote_copy(
            src_ref=part.at[:, theirs, :],
            dst_ref=got.at[24 + groups - step],
            send_sem=part_send.at[step],
            recv_sem=part_recv.at[groups - step],
            device_id=(slab, group_at(step)),
            device_id_type=MESH,
        )

    def part_arrival(step):
        theirs = pl.ds(pl.multiple_of(group_at(step) * 16, 16), 16)
        return pltpu.make_async_remote_copy(
            src_ref=part.at[:, theirs, :],
            dst_ref=got.at[24 + step],
            send_sem=part_send.at[step],
            recv_sem=part_recv.at[step],
            device_id=(slab, group_at(step)),
            device_id_type=MESH,
        )

    for step in range(1, groups):
        part_copy(step).start()
    share = jnp.stack([adding[pl.ds(pl.multiple_of(128 * i + group * 16, 16), 16), :] for i in range(3)])
    for step in range(1, groups):
        part_arrival(step).wait_recv()
        share = share + got[24 + step].astype(F32)
    halves[:, mine, :] = share.astype(BF)
    for step in range(1, groups):
        half_copy(step).start()
    for step in range(1, groups):
        half_arrival(step).wait_recv()
    for i in range(3):
        out[i] = state[i] + halves[i].astype(F32)

    def end_force(k, carry):
        force_copy(k).wait_send()
        return carry

    def end_far(q, carry):
        ask_copy(q).wait_send()
        ans_copy(q).wait_send()
        give_copy(q).wait_send()
        return carry

    def end_near(step, carry):
        sum_copy(step).wait_send()
        part_copy(step).wait_send()
        half_copy(step).wait_send()
        return carry

    to_above.wait_send()
    to_below.wait_send()
    lax.fori_loop(0, 23, end_force, 0)
    lax.fori_loop(1, 16, end_far, 0)
    lax.fori_loop(1, groups, end_near, 0)


def body(
    disp_now, disp_prev, inv_mass, cell_nodes, shape_grads, cell_weights, cell_shear, cell_bulk,
    block_owner, block_nodes, block_phi, block_corr, block_target, block_fixed,
):
    vmem = pl.BlockSpec(memory_space=pltpu.VMEM)
    anywhere = pl.BlockSpec(memory_space=pl.ANY)
    dma = pltpu.SemaphoreType.DMA
    message = pltpu.VMEM((16, 16, 256), BF)
    nodal = pltpu.VMEM((3, 128, 256), BF)
    result = pl.pallas_call(
        step_kernel,
        name="step",
        out_shape=jax.ShapeDtypeStruct((3, 128, 256), F32),
        in_specs=[anywhere] * 3 + [vmem, anywhere] + [vmem] * 5 + [anywhere] * 2 + [vmem] * 2,
        out_specs=vmem,
        scratch_shapes=[
            pltpu.VMEM((3, 32768), F32),
            pltpu.VMEM((3, 32768), F32),
            pltpu.VMEM((256, 128), F32),
            pltpu.VMEM((3, 128, 256), F32),
            pltpu.VMEM((3, 384, 256), BF),
            pltpu.VMEM((8, 1, QUAD), jnp.int32),
            pltpu.VMEM((32, 3, 192, 128), BF),
            pltpu.VMEM((3, 128, 128), F32),
            pltpu.VMEM((8, 8, QUAD), F32),
            pltpu.VMEM((8, 3, 256, QUAD), BF),
            pltpu.VMEM((8, 384, QUAD), BF),
            pltpu.VMEM((3, 3, 128, 256), BF),
            pltpu.VMEM((32, 3, 16, 256), BF),
            nodal,
            message, message, message, message, message, message,
            pltpu.VMEM((384, 256), F32),
            nodal,
            nodal,
            pltpu.VMEM((16, 256, 256), F32),
            pltpu.VMEM((16, 256, 128), F32),
            pltpu.VMEM((16, 256, 256), BF),
            pltpu.VMEM((16, 256, 128), BF),
            pltpu.VMEM((128, 128), F32),
            pltpu.VMEM((128, 128), F32),
            pltpu.VMEM((2, 128, 128), F32),
            pltpu.VMEM((128, 256), F32),
            pltpu.VMEM((128, 128), F32),
            pltpu.VMEM((256, 256), BF),
            pltpu.VMEM((384, 256), BF),
            pltpu.VMEM((16, 256, 1024), BF),
            dma((6,)), dma((3,)), dma((3,)), dma((23,)), dma((23,)), dma((8,)), dma((8,)), dma((16,)), dma((16,)),
            dma((16,)), dma((16,)), dma((16,)), dma((16,)), dma((8,)), dma((8,)), dma((8,)), dma((8,)),
        ],
        compiler_params=pltpu.CompilerParams(
            vmem_limit_bytes=58 << 20, collective_id=0, has_side_effects=True
        ),
    )(
        disp_now,
        disp_prev,
        inv_mass.reshape(256, 128),
        cell_nodes,
        shape_grads,
        cell_weights,
        cell_shear.reshape(1, 32),
        cell_bulk.reshape(1, 32),
        block_owner.reshape(1, 32),
        block_nodes,
        block_phi.reshape(16, 256, 256),
        block_corr.reshape(16, 256, 128),
        jnp.moveaxis(block_target, 1, 0),
        block_fixed,
    )
    return result.reshape(3, 32768)


def solution(mesh):
    both = ("slab", "group")
    placed = (
        P(None, "slab"), P(None, "slab"), P("slab"), P(both, None), P(both, None, None, None), P(both, None),
        P(both), P(both), P(both, None), P(both, None), P(both, None, None), P(both, None, None),
        P(both, None, None), P(both, None),
    )
    return jax.shard_map(body, mesh=mesh, in_specs=placed, out_specs=P(None, "slab"), check_vma=False)
```

```python
import jax
import jax.numpy as jnp
from jax import lax
from jax.experimental import pallas as pl
from jax.experimental.pallas import tpu as pltpu
from jax.sharding import PartitionSpec as P

BF = jnp.bfloat16
F32 = jnp.float32
NT = (((1,), (1,)), ((), ()))
MESH = pl.DeviceIdType.MESH
CAP = 4
QUAD = 768


def onehot(index, size):
    rows = lax.broadcasted_iota(jnp.int32, (size, index.shape[1]), 0)
    return jnp.where(rows == index, 1.0, 0.0).astype(BF)


def step_kernel(
    now_hbm, prev_hbm, mass_hbm, cell_nodes, grads_hbm, weights, shear, bulk, owner, block_nodes, phi_hbm, corr_hbm,
    target, fixed, out,
    lines, prev, mass, state, tables, nodes, grads, field, near, columns, spread, forces, paired, merged,
    got, summed, asking, asked, answer, answered, giving, given, adding, part, halves,
    phi, corr, phi_bf, corr_bf, goal, held, numbers, values, resids, permuted, gathered, hots,
    load_sem, enter_sem, pair_send, pair_recv, halo_send, halo_recv, force_send, force_recv, all_send, all_recv, ask_send, ask_recv, ans_send, ans_recv,
    give_send, give_recv, part_send, part_recv, half_send, half_recv,
):
    slab, group = lax.axis_index("slab"), lax.axis_index("group")
    slabs, groups = 16, 8

    def slab_at(by):
        return lax.rem(slab + by + slabs, slabs)

    depth, core = group // 2, lax.rem(group, 2)
    depths = groups // 2
    sibling = (slab, depth * 2 + 1 - core)

    def depth_at(by):
        return lax.rem(depth + by, depths)

    def level(by):
        return depth_at(by) * 2 + core

    load_now = pltpu.make_async_copy(now_hbm, lines, load_sem.at[0])
    load_grads = pltpu.make_async_copy(grads_hbm, grads, load_sem.at[1])
    load_prev = pltpu.make_async_copy(prev_hbm, prev, load_sem.at[2])
    load_mass = pltpu.make_async_copy(mass_hbm, mass, load_sem.at[3])
    load_phi = pltpu.make_async_copy(phi_hbm, phi, load_sem.at[4])
    load_corr = pltpu.make_async_copy(corr_hbm, corr, load_sem.at[5])
    load_now.start()
    load_grads.start()
    load_prev.start()
    load_mass.start()
    load_phi.start()
    load_corr.start()

    barrier = pltpu.get_barrier_semaphore()

    def greet(device):
        pl.semaphore_signal(barrier, inc=1, device_id=device, device_id_type=MESH)

    def greet_again(device):
        pl.semaphore_signal(enter_sem, inc=1, device_id=device, device_id_type=MESH)

    for by in (1, 15, 4, 8, 12, 6, 10):
        greet((slab_at(by), group))
    for by in (1, 2, 3):
        greet((slab, level(by)))
    greet(sibling)

    def relaid(source, use):
        def move(block, carry):
            start = pl.multiple_of(block * 2048, 2048)
            wide = source[:, pl.ds(start, 2048)]
            at = pl.ds(pl.multiple_of(block * 8, 8), 8)
            for i in range(3):
                use(i, at, jnp.concatenate([wide[i : i + 1, 256 * r : 256 * r + 256] for r in range(8)], axis=0))
            return carry

        lax.fori_loop(0, 16, move, 0)

    def set_state(i, at, value):
        state[i, at, :] = value

    load_now.wait()
    relaid(lines, set_state)
    for i in range(3):
        tables[1, 128 * i : 128 * i + 128, :] = state[i].astype(BF)
    pl.semaphore_wait(barrier, 11)

    def halo(side, by):
        return pltpu.make_async_remote_copy(
            src_ref=tables.at[1],
            dst_ref=tables.at[side],
            send_sem=halo_send.at[side],
            recv_sem=halo_recv.at[side],
            device_id=(slab_at(by), group),
            device_id_type=MESH,
        )

    to_above, to_below = halo(0, 1), halo(2, -1)
    to_above.start()
    to_below.start()
    for by in (1, 15):
        greet_again((slab_at(by), group))
    for by in (1, 2, 3):
        greet_again((slab, level(by)))

    own_row = owner[...]
    diag = lax.broadcasted_iota(jnp.int32, (32, 32), 0) == lax.broadcasted_iota(jnp.int32, (32, 32), 1)
    own_col = jnp.sum(jnp.where(diag, own_row, 0), axis=1, keepdims=True)
    block_wide = lax.broadcasted_iota(jnp.int32, (32, 128), 0)
    of_lane = lax.broadcasted_iota(jnp.int32, (32, 128), 1) // 4
    own_wide = jnp.sum(jnp.where(block_wide == of_lane, own_col, 0), axis=0, keepdims=True)
    earlier = (own_col == own_wide) & (block_wide < of_lane)
    rank = jnp.sum(jnp.where(earlier, 1, 0), axis=0, keepdims=True)
    relative = own_wide - slab
    relative = jnp.where(relative < 0, relative + slabs, relative)
    key = relative * 16 + rank * 4 + lax.broadcasted_iota(jnp.int32, (1, 128), 1) % 4
    to_slots = onehot(key, 256)
    square = lax.broadcasted_iota(jnp.int32, (128, 128), 0) == lax.broadcasted_iota(jnp.int32, (128, 128), 1)
    key_col = jnp.sum(jnp.where(square, key, 0), axis=1, keepdims=True)

    node = block_nodes[...]
    numbers[...] = jnp.zeros_like(numbers)
    for side in range(2):
        span = slice(128 * side, 128 * side + 128)
        numbers[side, pl.ds(0, 32, stride=4), :] = ((node[:, span] >> 8) + 1).astype(F32)
        numbers[side, pl.ds(1, 32, stride=4), :] = ((node[:, span] & 255) + 1).astype(F32)
    named = jnp.concatenate([numbers[0], numbers[1]], axis=1).astype(BF)
    asks = jnp.dot(to_slots, named, preferred_element_type=F32) - 1.0
    for q in range(16):
        asking[q] = asks[16 * q : 16 * q + 16].astype(BF)

    def exchange(source, landing, send, recv):
        def copy(q):
            return pltpu.make_async_remote_copy(
                src_ref=source.at[q],
                dst_ref=landing.at[slabs - q],
                send_sem=send.at[q],
                recv_sem=recv.at[slabs - q],
                device_id=(slab_at(q), group),
                device_id_type=MESH,
            )

        def arrival(q):
            return pltpu.make_async_remote_copy(
                src_ref=source.at[q],
                dst_ref=landing.at[q],
                send_sem=send.at[q],
                recv_sem=recv.at[q],
                device_id=(slab_at(q), group),
                device_id_type=MESH,
            )

        return copy, arrival

    ask_copy, ask_arrival = exchange(asking, asked, ask_send, ask_recv)
    ans_copy, ans_arrival = exchange(answer, answered, ans_send, ans_recv)
    give_copy, give_arrival = exchange(giving, given, give_send, give_recv)

    def start_ask(q, carry):
        ask_copy(q).start()
        return carry

    pl.semaphore_wait(enter_sem, 5)
    lax.fori_loop(1, 16, start_ask, 0, unroll=3)
    asked[0] = asking[0]

    def flatten(quad, carry):
        rows = [cell_nodes[pl.ds(4 * quad + e, 1), :] for e in range(4)]
        nodes[quad] = jnp.concatenate(rows, axis=1)
        return carry

    lax.fori_loop(0, 8, flatten, 0)
    rows_quad = lax.broadcasted_iota(jnp.int32, (128, QUAD), 0)

    def pick(total, row):
        mask = rows_quad == row
        return [
            jnp.sum(jnp.where(mask, total[128 * i : 128 * i + 128], 0.0), axis=0, keepdims=True) for i in range(3)
        ]

    def gather_own(quad, carry):
        number = nodes[quad]
        side_of, row, column = number >> 15, (number >> 8) & 127, number & 255
        for side in range(3):
            columns[quad, side] = onehot(jnp.where(side_of == side, column, -1), 256)
        total = jnp.dot(tables[1], columns[quad, 1], preferred_element_type=F32)
        for i, line in enumerate(pick(total, row)):
            near[quad, i : i + 1, :] = line
        return carry

    lax.fori_loop(0, 8, gather_own, 0, unroll=2)
    load_prev.wait()

    def set_base(i, at, value):
        state[i, at, :] = 2.0 * state[i, at, :] - value

    relaid(prev, set_base)
    to_above.wait_recv()
    to_below.wait_recv()
    tables[0] = jnp.where(slab == 0, 0.0, tables[0].astype(F32)).astype(BF)
    tables[2] = jnp.where(slab == slabs - 1, 0.0, tables[2].astype(F32)).astype(BF)

    def gather_sides(quad, carry):
        row = (nodes[quad] >> 8) & 127
        total = jnp.dot(tables[0], columns[quad, 0], preferred_element_type=F32)
        total += jnp.dot(tables[2], columns[quad, 2], preferred_element_type=F32)
        for i, line in enumerate(pick(total, row)):
            near[quad, i : i + 1, :] += line
        return carry

    lax.fori_loop(0, 8, gather_sides, 0, unroll=2)
    load_grads.wait()
    sub = lax.broadcasted_iota(jnp.int32, (8, 384), 0)
    lane = lax.broadcasted_iota(jnp.int32, (8, 384), 1)
    own = (sub >= 4) == (lane >= 192)

    def gradient(quad, carry):
        for pair in range(2):
            left = jnp.zeros((8, 384), F32)
            for i in range(3):
                left = jnp.where(sub % 4 == i, near[quad, i : i + 1, 384 * pair : 384 * pair + 384], left)
            left = jnp.where(own, left, 0.0).astype(BF)
            for j in range(3):
                first = 4 * quad + 2 * pair
                both = jnp.concatenate([grads[first, j], grads[first + 1, j]], axis=0)
                at = pl.ds(pl.multiple_of(16 * quad + 8 * pair, 8), 8)
                field[j, at, :] = jnp.dot(left, both, preferred_element_type=F32)
        return carry

    lax.fori_loop(0, 8, gradient, 0, unroll=2)
    full = [
        [field[j, pl.ds(i, 32, stride=4), :] + (1.0 if i == j else 0.0) for j in range(3)]
        for i in range(3)
    ]
    cofactor = [
        [
            full[(i + 1) % 3][(j + 1) % 3] * full[(i + 2) % 3][(j + 2) % 3]
            - full[(i + 1) % 3][(j + 2) % 3] * full[(i + 2) % 3][(j + 1) % 3]
            for j in range(3)
        ]
        for i in range(3)
    ]
    volume = full[0][0] * cofactor[0][0] + full[0][1] * cofactor[0][1] + full[0][2] * cofactor[0][2]
    clamped = jnp.maximum(volume, 0.3)
    mu = jnp.sum(jnp.where(diag, shear[...], 0.0), axis=1, keepdims=True)
    lam = jnp.sum(jnp.where(diag, bulk[...], 0.0), axis=1, keepdims=True)
    weight = weights[...]
    factor = (lam * jnp.log(clamped) - mu) / clamped
    for i in range(3):
        for j in range(3):
            field[j, pl.ds(i, 32, stride=4), :] = weight * (mu * full[i][j] + factor * cofactor[i][j])
    low_lane = lax.broadcasted_iota(jnp.int32, (1, 384), 1) < 192
    rows_pair = lax.broadcasted_iota(jnp.int32, (128, 384), 0)

    def cell_forces(quad, carry):
        for pair in range(2):
            total = None
            for j in range(3):
                first = 4 * quad + 2 * pair
                at = pl.ds(pl.multiple_of(16 * quad + 8 * pair, 8), 8)
                both = jnp.concatenate([grads[first, j], grads[first + 1, j]], axis=0)
                piece = lax.dot_general(field[j, at, :].astype(BF), both, NT, preferred_element_type=F32)
                total = piece if total is None else total + piece
            span = slice(384 * pair, 384 * pair + 384)
            mask = rows_pair == ((nodes[quad, :, span] >> 8) & 127)
            for i in range(3):
                value = jnp.where(low_lane, total[i : i + 1], total[4 + i : 5 + i])
                spread[quad, 128 * i : 128 * i + 128, span] = jnp.where(mask, value, 0.0).astype(BF)
        return carry

    lax.fori_loop(0, 8, cell_forces, 0, unroll=2)

    def pair_copy(side):
        return pltpu.make_async_remote_copy(
            src_ref=forces.at[side, :, :, 1 - core],
            dst_ref=paired.at[side],
            send_sem=pair_send.at[side],
            recv_sem=pair_recv.at[side],
            device_id=sibling,
            device_id_type=MESH,
        )

    def force_copy(k):
        source, shift, by = ((0, -1, k), (2, 1, k - 4), (1, 0, k - 7))[k // 4]
        return pltpu.make_async_remote_copy(
            src_ref=merged.at[source, :, depth_at(by)],
            dst_ref=got.at[k],
            send_sem=force_send.at[k],
            recv_sem=force_recv.at[k],
            device_id=(slab_at(shift), level(by)),
            device_id_type=MESH,
        )

    def scatter(side):
        total = None
        for quad in range(8):
            piece = lax.dot_general(spread[quad], columns[quad, side], NT, preferred_element_type=F32)
            total = piece if total is None else total + piece
        for i in range(3):
            forces[side, i] = total[128 * i : 128 * i + 128].reshape(4, 2, 16, 256).astype(BF)
        pair_copy(side).start()

    def merge(side, first, last):
        pair_copy(side).wait_recv()
        for i in range(3):
            merged[side, i] = (forces[side, i, :, core].astype(F32) + paired[side, i].astype(F32)).astype(BF)
        for k in range(first, last):
            force_copy(k).start()

    scatter(0)
    scatter(2)
    merge(0, 0, 4)
    scatter(1)
    merge(2, 4, 8)

    def spots(q):
        spot = asked[q].astype(F32)
        row = jnp.concatenate([spot[4 * c : 4 * c + 1] for c in range(CAP)], axis=1).astype(jnp.int32)
        column = jnp.concatenate([spot[4 * c + 1 : 4 * c + 2] for c in range(CAP)], axis=1).astype(jnp.int32)
        return row, column

    def heat(q):
        hots[q] = onehot(spots(q)[1], 256)

    def heat_far(q, carry):
        ask_arrival(q).wait_recv()
        heat(q)
        return carry

    heat(0)
    lax.fori_loop(1, 4, heat_far, 0, unroll=3)
    merge(1, 8, 11)
    lax.fori_loop(4, 16, heat_far, 0, unroll=3)
    for i in range(3):
        goal[pl.ds(i, 32, stride=4), :] = target[i]
    goal[pl.ds(3, 32, stride=4), :] = jnp.zeros((32, 128), F32)
    for i in range(4):
        held[pl.ds(i, 32, stride=4), :] = fixed[...].astype(F32)
    load_phi.wait()
    load_corr.wait()

    def narrow(pair, carry):
        phi_bf[pair] = phi[pair].astype(BF)
        corr_bf[pair] = corr[pair].astype(BF)
        return carry

    lax.fori_loop(0, 16, narrow, 0)
    load_mass.wait()

    share = merged[1, :, depth].astype(F32)
    for k in range(11):
        force_copy(k).wait_recv()
        piece = got[k].astype(F32)
        if k < 4:
            piece = jnp.where(slab == slabs - 1, 0.0, piece)
        elif k < 8:
            piece = jnp.where(slab == 0, 0.0, piece)
        share = share + piece

    def shared(buffer, send, recv):
        def copy(by):
            return pltpu.make_async_remote_copy(
                src_ref=buffer.at[:, group],
                dst_ref=buffer.at[:, group],
                send_sem=send.at[by],
                recv_sem=recv.at[depths - by],
                device_id=(slab, level(by)),
                device_id_type=MESH,
            )

        def arrival(by):
            return pltpu.make_async_remote_copy(
                src_ref=buffer.at[:, level(by)],
                dst_ref=buffer.at[:, level(by)],
                send_sem=send.at[by],
                recv_sem=recv.at[by],
                device_id=(slab, level(by)),
                device_id_type=MESH,
            )

        def cross(by):
            return pltpu.make_async_remote_copy(
                src_ref=buffer.at[:, level(by)],
                dst_ref=buffer.at[:, level(by)],
                send_sem=send.at[depths + by],
                recv_sem=recv.at[depths + by],
                device_id=sibling,
                device_id_type=MESH,
            )

        def crossed(by):
            other = depth_at(by) * 2 + 1 - core
            return pltpu.make_async_remote_copy(
                src_ref=buffer.at[:, other],
                dst_ref=buffer.at[:, other],
                send_sem=send.at[depths + by],
                recv_sem=recv.at[depths + by],
                device_id=sibling,
                device_id_type=MESH,
            )

        def begin():
            for by in (2, 1, 3):
                copy(by).start()
            cross(0).start()

        def finish():
            for by in (1, 3, 2):
                arrival(by).wait_recv()
                cross(by).start()
            for by in (0, 1, 3, 2):
                crossed(by).wait_recv()

        def close():
            for by in (1, 2, 3):
                copy(by).wait_send()
            for by in range(4):
                cross(by).wait_send()

        return begin, finish, close

    sum_begin, sum_finish, sum_close = shared(summed, all_send, all_recv)
    half_begin, half_finish, half_close = shared(halves, half_send, half_recv)
    summed[:, group] = share.astype(BF)
    sum_begin()
    scale = jnp.concatenate([mass[pl.ds(0, 128, stride=2), :], mass[pl.ds(1, 128, stride=2), :]], axis=1)
    sum_finish()
    for i in range(3):
        state[i] = state[i] - scale * summed[i].reshape(128, 256).astype(F32)
        gathered[128 * i : 128 * i + 128, :] = state[i].astype(BF)

    rows_of = lax.broadcasted_iota(jnp.int32, (128, 1024), 0)
    sixteen = lax.broadcasted_iota(jnp.int32, (16, 256), 0)

    def look(q):
        row, _ = spots(q)
        hit = jnp.dot(gathered[...], hots[q], preferred_element_type=F32)
        mask = rows_of == row
        found = jnp.zeros((16, 256), F32)
        for i in range(3):
            line = jnp.sum(jnp.where(mask, hit[128 * i : 128 * i + 128], 0.0), axis=0, keepdims=True)
            for c in range(CAP):
                found = jnp.where(sixteen == 4 * c + i, line[:, 256 * c : 256 * c + 256], found)
        answer[q] = found.astype(BF)

    def look_far(q, carry):
        look(q)
        ans_copy(q).start()
        return carry

    lax.fori_loop(1, 16, look_far, 0, unroll=3)
    look(0)
    permuted[0:16] = answer[0]
    to_blocks = jnp.where(lax.broadcasted_iota(jnp.int32, (128, 256), 1) == key_col, 1.0, 0.0).astype(BF)

    def take(q, carry):
        ans_arrival(q).wait_recv()
        permuted[pl.ds(pl.multiple_of(q * 16, 16), 16), :] = answered[q]
        return carry

    lax.fori_loop(1, 16, take, 0, unroll=3)
    values[...] = jnp.dot(to_blocks, permuted[...], preferred_element_type=F32)

    upper = lax.broadcasted_iota(jnp.int32, (8, 128), 0) < 4

    def at_pair(pair):
        return pl.ds(pl.multiple_of(8 * pair, 8), 8)

    def residual(pair, carry):
        at = at_pair(pair)
        both = lax.dot_general(values[at, :].astype(BF), phi_bf[pair], NT, preferred_element_type=F32)
        interp = jnp.where(upper, both[:, :128], both[:, 128:])
        resids[at, :] = held[at, :] * (goal[at, :] - interp)
        return carry

    def correction(pair, carry):
        at = at_pair(pair)
        both = lax.dot_general(resids[at, :].astype(BF), corr_bf[pair], NT, preferred_element_type=F32)
        values[at, 0:128] = jnp.where(upper, both[:, :128], 0.0)
        values[at, 128:256] = jnp.where(upper, 0.0, both[:, 128:])
        return carry

    def spreading(pair, carry):
        at = at_pair(pair)
        values[at, :] = jnp.dot(values[at, :].astype(BF), phi_bf[pair], preferred_element_type=F32)
        return carry

    lax.fori_loop(0, 16, residual, 0, unroll=8)
    lax.fori_loop(0, 16, correction, 0, unroll=8)
    lax.fori_loop(0, 16, spreading, 0, unroll=8)
    gives = jnp.dot(to_slots, values[...].astype(BF), preferred_element_type=F32).astype(BF)
    for q in range(16):
        giving[q] = gives[16 * q : 16 * q + 16]

    def start_give(q, carry):
        give_copy(q).start()
        return carry

    lax.fori_loop(1, 16, start_give, 0, unroll=3)
    given[0] = giving[0]

    def place(q):
        row, _ = spots(q)
        mask = rows_of == row
        amount = given[q].astype(F32)
        rows = []
        for i in range(3):
            line = jnp.concatenate([amount[4 * c + i : 4 * c + i + 1] for c in range(CAP)], axis=1)
            rows.append(jnp.where(mask, line, 0.0).astype(BF))
        return lax.dot_general(jnp.concatenate(rows, axis=0), hots[q], NT, preferred_element_type=F32)

    adding[...] = place(0)

    def place_far(third, carry):
        total = None
        for c in range(3):
            q = 3 * third + 1 + c
            give_arrival(q).wait_recv()
            piece = place(q)
            total = piece if total is None else total + piece
        adding[...] += total
        return carry

    lax.fori_loop(0, 5, place_far, 0)

    part_out = pltpu.make_async_remote_copy(
        src_ref=part.at[:, :, 1 - core],
        dst_ref=paired.at[3],
        send_sem=pair_send.at[3],
        recv_sem=pair_recv.at[3],
        device_id=sibling,
        device_id_type=MESH,
    )
    for i in range(3):
        part[i] = adding[128 * i : 128 * i + 128, :].reshape(4, 2, 16, 256).astype(BF)
    part_out.start()

    def part_copy(by):
        return pltpu.make_async_remote_copy(
            src_ref=merged.at[3, :, depth_at(by)],
            dst_ref=got.at[11 + depths - by],
            send_sem=part_send.at[by],
            recv_sem=part_recv.at[depths - by],
            device_id=(slab, level(by)),
            device_id_type=MESH,
        )

    def part_arrival(by):
        return pltpu.make_async_remote_copy(
            src_ref=merged.at[3, :, depth_at(by)],
            dst_ref=got.at[11 + by],
            send_sem=part_send.at[by],
            recv_sem=part_recv.at[by],
            device_id=(slab, level(by)),
            device_id_type=MESH,
        )

    part_out.wait_recv()
    for i in range(3):
        merged[3, i] = (part[i, :, core].astype(F32) + paired[3, i].astype(F32)).astype(BF)
    for by in (2, 1, 3):
        part_copy(by).start()
    share = merged[3, :, depth].astype(F32)
    for by in (1, 3, 2):
        part_arrival(by).wait_recv()
        share = share + got[11 + by].astype(F32)
    halves[:, group] = share.astype(BF)
    half_begin()
    half_finish()
    for i in range(3):
        out[i] = state[i] + halves[i].reshape(128, 256).astype(F32)

    def end_far(q, carry):
        ask_copy(q).wait_send()
        ans_copy(q).wait_send()
        give_copy(q).wait_send()
        return carry

    to_above.wait_send()
    to_below.wait_send()
    for side in range(3):
        pair_copy(side).wait_send()
    for k in range(11):
        force_copy(k).wait_send()
    lax.fori_loop(1, 16, end_far, 0)
    sum_close()
    part_out.wait_send()
    for by in (1, 2, 3):
        part_copy(by).wait_send()
    half_close()


def body(
    disp_now, disp_prev, inv_mass, cell_nodes, shape_grads, cell_weights, cell_shear, cell_bulk,
    block_owner, block_nodes, block_phi, block_corr, block_target, block_fixed,
):
    vmem = pl.BlockSpec(memory_space=pltpu.VMEM)
    anywhere = pl.BlockSpec(memory_space=pl.ANY)
    dma = pltpu.SemaphoreType.DMA
    message = pltpu.VMEM((16, 16, 256), BF)
    nodal = pltpu.VMEM((3, 8, 16, 256), BF)
    paired = pltpu.VMEM((4, 3, 4, 16, 256), BF)
    result = pl.pallas_call(
        step_kernel,
        name="step",
        out_shape=jax.ShapeDtypeStruct((3, 128, 256), F32),
        in_specs=[anywhere] * 3 + [vmem, anywhere] + [vmem] * 5 + [anywhere] * 2 + [vmem] * 2,
        out_specs=vmem,
        scratch_shapes=[
            pltpu.VMEM((3, 32768), F32),
            pltpu.VMEM((3, 32768), F32),
            pltpu.VMEM((256, 128), F32),
            pltpu.VMEM((3, 128, 256), F32),
            pltpu.VMEM((3, 384, 256), BF),
            pltpu.VMEM((8, 1, QUAD), jnp.int32),
            pltpu.VMEM((32, 3, 192, 128), BF),
            pltpu.VMEM((3, 128, 128), F32),
            pltpu.VMEM((8, 8, QUAD), F32),
            pltpu.VMEM((8, 3, 256, QUAD), BF),
            pltpu.VMEM((8, 384, QUAD), BF),
            pltpu.VMEM((3, 3, 4, 2, 16, 256), BF),
            paired,
            paired,
            pltpu.VMEM((15, 3, 16, 256), BF),
            nodal,
            message, message, message, message, message, message,
            pltpu.VMEM((384, 256), F32),
            pltpu.VMEM((3, 4, 2, 16, 256), BF),
            nodal,
            pltpu.VMEM((16, 256, 256), F32),
            pltpu.VMEM((16, 256, 128), F32),
            pltpu.VMEM((16, 256, 256), BF),
            pltpu.VMEM((16, 256, 128), BF),
            pltpu.VMEM((128, 128), F32),
            pltpu.VMEM((128, 128), F32),
            pltpu.VMEM((2, 128, 128), F32),
            pltpu.VMEM((128, 256), F32),
            pltpu.VMEM((128, 128), F32),
            pltpu.VMEM((256, 256), BF),
            pltpu.VMEM((384, 256), BF),
            pltpu.VMEM((16, 256, 1024), BF),
            dma((6,)), pltpu.SemaphoreType.REGULAR, dma((4,)), dma((4,)), dma((3,)), dma((3,)), dma((11,)), dma((11,)),
            dma((8,)), dma((8,)), dma((16,)), dma((16,)), dma((16,)), dma((16,)), dma((16,)), dma((16,)), dma((4,)),
            dma((4,)), dma((8,)), dma((8,)),
        ],
        compiler_params=pltpu.CompilerParams(
            vmem_limit_bytes=46 << 20, collective_id=0, has_side_effects=True
        ),
    )(
        disp_now,
        disp_prev,
        inv_mass.reshape(256, 128),
        cell_nodes,
        shape_grads,
        cell_weights,
        cell_shear.reshape(1, 32),
        cell_bulk.reshape(1, 32),
        block_owner.reshape(1, 32),
        block_nodes,
        block_phi.reshape(16, 256, 256),
        block_corr.reshape(16, 256, 128),
        jnp.moveaxis(block_target, 1, 0),
        block_fixed,
    )
    return result.reshape(3, 32768)


def solution(mesh):
    both = ("slab", "group")
    placed = (
        P(None, "slab"), P(None, "slab"), P("slab"), P(both, None), P(both, None, None, None), P(both, None),
        P(both), P(both), P(both, None), P(both, None), P(both, None, None), P(both, None, None),
        P(both, None, None), P(both, None),
    )
    return jax.shard_map(body, mesh=mesh, in_specs=placed, out_specs=P(None, "slab"), check_vma=False)
```

```python
import jax
import jax.numpy as jnp
from jax import lax
from jax.experimental import pallas as pl
from jax.experimental.pallas import tpu as pltpu
from jax.sharding import PartitionSpec as P

BF = jnp.bfloat16
F32 = jnp.float32
NT = (((1,), (1,)), ((), ()))
MESH = pl.DeviceIdType.MESH
CAP = 4
QUAD = 768
FAR = tuple(range(1, 16))
NEAR = FAR


def onehot(index, size):
    rows = lax.broadcasted_iota(jnp.int32, (size, index.shape[1]), 0)
    return jnp.where(rows == index, 1.0, 0.0).astype(BF)


def step_kernel(
    now_hbm, prev_hbm, mass_hbm, cell_nodes, grads_hbm, weights, shear, bulk, owner, block_nodes, phi_hbm, corr_hbm,
    target, fixed, out,
    lines, prev, mass, state, tables, nodes, grads, field, near, columns, spread, forces, paired, merged, pooled,
    got, summed, asking, asked, answer, answered, giving, given, adding, part, halves,
    phi, corr, phi_bf, corr_bf, goal, held, numbers, values, resids, gathered, hots,
    load_sem, enter_sem, pair_send, pair_recv, halo_send, halo_recv, force_send, force_recv, all_send, all_recv, ask_send, ask_recv, ans_send, ans_recv,
    give_send, give_recv, part_send, part_recv, half_send, half_recv,
):
    slab, group = lax.axis_index("slab"), lax.axis_index("group")
    slabs, groups = 16, 8

    def slab_at(by):
        return lax.rem(slab + by + slabs, slabs)

    depth, core = group // 2, lax.rem(group, 2)
    depths = groups // 2
    sibling = (slab, depth * 2 + 1 - core)

    def depth_at(by):
        return lax.rem(depth + by, depths)

    def level(by):
        return depth_at(by) * 2 + core

    def group_at(by):
        return lax.rem(group + by, groups)

    load_now = pltpu.make_async_copy(now_hbm, lines, load_sem.at[0])
    load_grads = pltpu.make_async_copy(grads_hbm, grads, load_sem.at[1])
    load_prev = pltpu.make_async_copy(prev_hbm, prev, load_sem.at[2])
    load_mass = pltpu.make_async_copy(mass_hbm, mass, load_sem.at[3])
    load_phi = pltpu.make_async_copy(phi_hbm, phi, load_sem.at[4])
    load_corr = pltpu.make_async_copy(corr_hbm, corr, load_sem.at[5])
    load_now.start()
    load_grads.start()
    load_prev.start()
    load_mass.start()
    load_phi.start()
    load_corr.start()

    barrier = pltpu.get_barrier_semaphore()

    def greet(device):
        pl.semaphore_signal(barrier, inc=1, device_id=device, device_id_type=MESH)

    def greet_again(device):
        pl.semaphore_signal(enter_sem, inc=1, device_id=device, device_id_type=MESH)

    for by in (1, 15, 4, 8, 12, 6, 10):
        greet((slab_at(by), group))
    for by in (1, 2, 3):
        greet((slab, level(by)))
    greet(sibling)

    def relaid(source, use):
        def move(block, carry):
            start = pl.multiple_of(block * 2048, 2048)
            wide = source[:, pl.ds(start, 2048)]
            at = pl.ds(pl.multiple_of(block * 8, 8), 8)
            for i in range(3):
                use(i, at, jnp.concatenate([wide[i : i + 1, 256 * r : 256 * r + 256] for r in range(8)], axis=0))
            return carry

        lax.fori_loop(0, 16, move, 0)

    def set_state(i, at, value):
        state[i, at, :] = value

    load_now.wait()
    relaid(lines, set_state)
    for i in range(3):
        tables[1, 128 * i : 128 * i + 128, :] = state[i].astype(BF)
    pl.semaphore_wait(barrier, 11)

    def halo(side, by):
        return pltpu.make_async_remote_copy(
            src_ref=tables.at[1],
            dst_ref=tables.at[side],
            send_sem=halo_send.at[side],
            recv_sem=halo_recv.at[side],
            device_id=(slab_at(by), group),
            device_id_type=MESH,
        )

    to_above, to_below = halo(0, 1), halo(2, -1)
    has_below, has_above = slab > 0, slab < slabs - 1
    pl.when(has_above)(to_above.start)
    pl.when(has_below)(to_below.start)
    for by in (1, 15):
        greet_again((slab_at(by), group))
    for by in (1, 2, 3):
        greet_again((slab, level(by)))

    own_row = owner[...]
    diag = lax.broadcasted_iota(jnp.int32, (32, 32), 0) == lax.broadcasted_iota(jnp.int32, (32, 32), 1)
    own_col = jnp.sum(jnp.where(diag, own_row, 0), axis=1, keepdims=True)
    block_wide = lax.broadcasted_iota(jnp.int32, (32, 128), 0)
    of_lane = lax.broadcasted_iota(jnp.int32, (32, 128), 1) // 4
    own_wide = jnp.sum(jnp.where(block_wide == of_lane, own_col, 0), axis=0, keepdims=True)
    earlier = (own_col == own_wide) & (block_wide < of_lane)
    rank = jnp.sum(jnp.where(earlier, 1, 0), axis=0, keepdims=True)
    relative = own_wide - slab
    relative = jnp.where(relative < 0, relative + slabs, relative)
    key = relative * 16 + rank * 4 + lax.broadcasted_iota(jnp.int32, (1, 128), 1) % 4
    to_slots = onehot(key, 256)
    square = lax.broadcasted_iota(jnp.int32, (128, 128), 0) == lax.broadcasted_iota(jnp.int32, (128, 128), 1)
    key_col = jnp.sum(jnp.where(square, key, 0), axis=1, keepdims=True)

    node = block_nodes[...]
    numbers[...] = jnp.zeros_like(numbers)
    for side in range(2):
        span = slice(128 * side, 128 * side + 128)
        numbers[side, pl.ds(0, 32, stride=4), :] = ((node[:, span] >> 8) + 1).astype(F32)
        numbers[side, pl.ds(1, 32, stride=4), :] = ((node[:, span] & 255) + 1).astype(F32)
    named = jnp.concatenate([numbers[0], numbers[1]], axis=1).astype(BF)
    asks = jnp.dot(to_slots, named, preferred_element_type=F32) - 1.0
    asking[...] = asks.astype(BF).reshape(16, 16, 256)

    def exchange(source, landing, send, recv):
        def copy(q):
            return pltpu.make_async_remote_copy(
                src_ref=source.at[q],
                dst_ref=landing.at[slabs - q],
                send_sem=send.at[q],
                recv_sem=recv.at[slabs - q],
                device_id=(slab_at(q), group),
                device_id_type=MESH,
            )

        def arrival(q):
            return pltpu.make_async_remote_copy(
                src_ref=source.at[q],
                dst_ref=landing.at[q],
                send_sem=send.at[q],
                recv_sem=recv.at[q],
                device_id=(slab_at(q), group),
                device_id_type=MESH,
            )

        return copy, arrival

    def ordered(order, turn, c):
        q = order[c]
        for t in range(1, 3):
            q = jnp.where(turn == t, order[5 * t + c], q)
        return q

    ask_copy, ask_arrival = exchange(asking, asked, ask_send, ask_recv)
    ans_copy, ans_arrival = exchange(answer, answered, ans_send, ans_recv)
    give_copy, give_arrival = exchange(giving, given, give_send, give_recv)

    pl.semaphore_wait(enter_sem, 5)
    for q in FAR:
        ask_copy(q).start()
    asked[0] = asking[0]

    def flatten(quad, carry):
        rows = [cell_nodes[pl.ds(4 * quad + e, 1), :] for e in range(4)]
        nodes[quad] = jnp.concatenate(rows, axis=1)
        return carry

    lax.fori_loop(0, 8, flatten, 0)
    rows_quad = lax.broadcasted_iota(jnp.int32, (128, QUAD), 0)

    def pick(total, row):
        mask = rows_quad == row
        return [
            jnp.sum(jnp.where(mask, total[128 * i : 128 * i + 128], 0.0), axis=0, keepdims=True) for i in range(3)
        ]

    def gather_own(quad, carry):
        number = nodes[quad]
        side_of, row, column = number >> 15, (number >> 8) & 127, number & 255
        for side in range(3):
            columns[quad, side] = onehot(jnp.where(side_of == side, column, -1), 256)
        total = jnp.dot(tables[1], columns[quad, 1], preferred_element_type=F32)
        for i, line in enumerate(pick(total, row)):
            near[quad, i : i + 1, :] = line
        return carry

    lax.fori_loop(0, 8, gather_own, 0, unroll=2)
    load_prev.wait()

    def set_base(i, at, value):
        state[i, at, :] = 2.0 * state[i, at, :] - value

    relaid(prev, set_base)
    def absent(side):
        tables[side] = jnp.zeros((384, 256), BF)

    pl.when(has_below)(to_above.wait_recv)
    pl.when(has_above)(to_below.wait_recv)
    pl.when(slab == 0)(lambda: absent(0))
    pl.when(slab == slabs - 1)(lambda: absent(2))

    def gather_sides(quad, carry):
        row = (nodes[quad] >> 8) & 127
        total = jnp.dot(tables[0], columns[quad, 0], preferred_element_type=F32)
        total += jnp.dot(tables[2], columns[quad, 2], preferred_element_type=F32)
        for i, line in enumerate(pick(total, row)):
            near[quad, i : i + 1, :] += line
        return carry

    lax.fori_loop(0, 8, gather_sides, 0, unroll=4)
    load_grads.wait()
    sub = lax.broadcasted_iota(jnp.int32, (8, 384), 0)
    lane = lax.broadcasted_iota(jnp.int32, (8, 384), 1)
    own = (sub >= 4) == (lane >= 192)

    def gradient(quad, carry):
        for pair in range(2):
            left = jnp.zeros((8, 384), F32)
            for i in range(3):
                left = jnp.where(sub % 4 == i, near[quad, i : i + 1, 384 * pair : 384 * pair + 384], left)
            left = jnp.where(own, left, 0.0).astype(BF)
            for j in range(3):
                first = 4 * quad + 2 * pair
                both = jnp.concatenate([grads[first, j], grads[first + 1, j]], axis=0)
                at = pl.ds(pl.multiple_of(16 * quad + 8 * pair, 8), 8)
                field[j, at, :] = jnp.dot(left, both, preferred_element_type=F32)
        return carry

    lax.fori_loop(0, 8, gradient, 0, unroll=4)
    full = [
        [field[j, pl.ds(i, 32, stride=4), :] + (1.0 if i == j else 0.0) for j in range(3)]
        for i in range(3)
    ]
    cofactor = [
        [
            full[(i + 1) % 3][(j + 1) % 3] * full[(i + 2) % 3][(j + 2) % 3]
            - full[(i + 1) % 3][(j + 2) % 3] * full[(i + 2) % 3][(j + 1) % 3]
            for j in range(3)
        ]
        for i in range(3)
    ]
    volume = full[0][0] * cofactor[0][0] + full[0][1] * cofactor[0][1] + full[0][2] * cofactor[0][2]
    clamped = jnp.maximum(volume, 0.3)
    mu = jnp.sum(jnp.where(diag, shear[...], 0.0), axis=1, keepdims=True)
    lam = jnp.sum(jnp.where(diag, bulk[...], 0.0), axis=1, keepdims=True)
    weight = weights[...]
    factor = (lam * jnp.log(clamped) - mu) / clamped
    for i in range(3):
        for j in range(3):
            field[j, pl.ds(i, 32, stride=4), :] = weight * (mu * full[i][j] + factor * cofactor[i][j])
    low_lane = lax.broadcasted_iota(jnp.int32, (1, 384), 1) < 192
    rows_pair = lax.broadcasted_iota(jnp.int32, (128, 384), 0)

    def cell_forces(quad, carry):
        for pair in range(2):
            total = None
            for j in range(3):
                first = 4 * quad + 2 * pair
                at = pl.ds(pl.multiple_of(16 * quad + 8 * pair, 8), 8)
                both = jnp.concatenate([grads[first, j], grads[first + 1, j]], axis=0)
                piece = lax.dot_general(field[j, at, :].astype(BF), both, NT, preferred_element_type=F32)
                total = piece if total is None else total + piece
            span = slice(384 * pair, 384 * pair + 384)
            mask = rows_pair == ((nodes[quad, :, span] >> 8) & 127)
            for i in range(3):
                value = jnp.where(low_lane, total[i : i + 1], total[4 + i : 5 + i])
                spread[quad, 128 * i : 128 * i + 128, span] = jnp.where(mask, value, 0.0).astype(BF)
        return carry

    lax.fori_loop(0, 8, cell_forces, 0, unroll=4)

    def pair_copy(side):
        return pltpu.make_async_remote_copy(
            src_ref=forces.at[side, :, :, 1 - core],
            dst_ref=paired.at[side],
            send_sem=pair_send.at[side],
            recv_sem=pair_recv.at[side],
            device_id=sibling,
            device_id_type=MESH,
        )

    def force_copy(k):
        source, shift, by = ((0, -1, k), (2, 1, k - 4), (1, 0, k - 7))[k // 4]
        return pltpu.make_async_remote_copy(
            src_ref=merged.at[source, :, depth_at(by)],
            dst_ref=got.at[k],
            send_sem=force_send.at[k],
            recv_sem=force_recv.at[k],
            device_id=(slab_at(shift), level(by)),
            device_id_type=MESH,
        )

    def scatter(side):
        total = None
        for quad in range(8):
            piece = lax.dot_general(spread[quad], columns[quad, side], NT, preferred_element_type=F32)
            total = piece if total is None else total + piece
        for i in range(3):
            forces[side, i] = total[128 * i : 128 * i + 128].reshape(4, 2, 16, 256).astype(BF)
        pair_copy(side).start()

    def merge(side, first, last):
        pair_copy(side).wait_recv()
        for i in range(3):
            merged[side, i] = (forces[side, i, :, core].astype(F32) + paired[side, i].astype(F32)).astype(BF)
        def leave():
            for k in range(first, last):
                force_copy(k).start()

        pl.when((has_below, slab >= 0, has_above)[side])(leave)

    scatter(0)
    scatter(2)
    merge(0, 0, 4)
    scatter(1)
    merge(2, 4, 8)

    def spots(q):
        spot = asked[q].astype(F32)
        row = jnp.concatenate([spot[4 * c : 4 * c + 1] for c in range(CAP)], axis=1).astype(jnp.int32)
        column = jnp.concatenate([spot[4 * c + 1 : 4 * c + 2] for c in range(CAP)], axis=1).astype(jnp.int32)
        return row, column

    def heat(q):
        hots[q] = onehot(spots(q)[1], 256)

    def heat_far(q, carry):
        ask_arrival(q).wait_recv()
        heat(q)
        return carry

    heat(0)
    merge(1, 8, 11)
    lax.fori_loop(1, 16, heat_far, 0, unroll=3)
    for i in range(3):
        goal[pl.ds(i, 32, stride=4), :] = target[i]
    goal[pl.ds(3, 32, stride=4), :] = jnp.zeros((32, 128), F32)
    for i in range(4):
        held[pl.ds(i, 32, stride=4), :] = fixed[...].astype(F32)
    load_phi.wait()
    load_corr.wait()

    def narrow(pair, carry):
        phi_bf[pair] = phi[pair].astype(BF)
        corr_bf[pair] = corr[pair].astype(BF)
        return carry

    lax.fori_loop(0, 16, narrow, 0)
    load_mass.wait()

    pooled[...] = merged[1, :, depth].astype(F32)

    def collect(first, last):
        value = pooled[...]
        for k in range(first, last):
            force_copy(k).wait_recv()
            value = value + got[k].astype(F32)
        pooled[...] = value

    collect(8, 11)
    pl.when(has_above)(lambda: collect(0, 4))
    pl.when(has_below)(lambda: collect(4, 8))

    def shared(buffer, send, recv):
        def copy(by):
            return pltpu.make_async_remote_copy(
                src_ref=buffer.at[:, group],
                dst_ref=buffer.at[:, group],
                send_sem=send.at[by],
                recv_sem=recv.at[groups - by],
                device_id=(slab, group_at(by)),
                device_id_type=MESH,
            )

        def arrival(by):
            return pltpu.make_async_remote_copy(
                src_ref=buffer.at[:, group_at(by)],
                dst_ref=buffer.at[:, group_at(by)],
                send_sem=send.at[by],
                recv_sem=recv.at[by],
                device_id=(slab, group_at(by)),
                device_id_type=MESH,
            )

        def begin():
            for by in (4, 3, 5, 2, 6, 1, 7):
                copy(by).start()

        def finish():
            for by in (1, 7, 2, 6, 3, 5, 4):
                arrival(by).wait_recv()

        def close():
            for by in range(1, groups):
                copy(by).wait_send()

        return begin, finish, close

    sum_begin, sum_finish, sum_close = shared(summed, all_send, all_recv)
    half_begin, half_finish, half_close = shared(halves, half_send, half_recv)
    summed[:, group] = pooled[...].astype(BF)
    sum_begin()
    scale = jnp.concatenate([mass[pl.ds(0, 128, stride=2), :], mass[pl.ds(1, 128, stride=2), :]], axis=1)
    sum_finish()
    for i in range(3):
        state[i] = state[i] - scale * summed[i].reshape(128, 256).astype(F32)
        gathered[128 * i : 128 * i + 128, :] = state[i].astype(BF)

    rows_of = lax.broadcasted_iota(jnp.int32, (128, 1024), 0)
    sixteen = lax.broadcasted_iota(jnp.int32, (16, 256), 0)

    def look(q):
        row, _ = spots(q)
        hit = jnp.dot(gathered[...], hots[q], preferred_element_type=F32)
        mask = rows_of == row
        found = jnp.zeros((16, 256), F32)
        for i in range(3):
            line = jnp.sum(jnp.where(mask, hit[128 * i : 128 * i + 128], 0.0), axis=0, keepdims=True)
            for c in range(CAP):
                found = jnp.where(sixteen == 4 * c + i, line[:, 256 * c : 256 * c + 256], found)
        return found.astype(BF)

    def look_far(turn, carry):
        for c in range(5):
            q = ordered(FAR, turn, c)
            answer[q] = look(q)
            ans_copy(q).start()
        return carry

    lax.fori_loop(0, 3, look_far, 0)
    answered[0] = look(0)
    to_blocks = jnp.where(lax.broadcasted_iota(jnp.int32, (128, 256), 1) == key_col, 1.0, 0.0).astype(BF)

    for q in NEAR:
        ans_arrival(q).wait_recv()
    values[...] = jnp.dot(to_blocks, answered[...].reshape(256, 256), preferred_element_type=F32)

    upper = lax.broadcasted_iota(jnp.int32, (8, 128), 0) < 4

    def at_pair(pair):
        return pl.ds(pl.multiple_of(8 * pair, 8), 8)

    def residual(pair, carry):
        at = at_pair(pair)
        both = lax.dot_general(values[at, :].astype(BF), phi_bf[pair], NT, preferred_element_type=F32)
        interp = jnp.where(upper, both[:, :128], both[:, 128:])
        resids[at, :] = held[at, :] * (goal[at, :] - interp)
        return carry

    def correction(pair, carry):
        at = at_pair(pair)
        both = lax.dot_general(resids[at, :].astype(BF), corr_bf[pair], NT, preferred_element_type=F32)
        values[at, 0:128] = jnp.where(upper, both[:, :128], 0.0)
        values[at, 128:256] = jnp.where(upper, 0.0, both[:, 128:])
        return carry

    def spreading(pair, carry):
        at = at_pair(pair)
        values[at, :] = jnp.dot(values[at, :].astype(BF), phi_bf[pair], preferred_element_type=F32)
        return carry

    lax.fori_loop(0, 16, residual, 0, unroll=8)
    lax.fori_loop(0, 16, correction, 0, unroll=8)
    lax.fori_loop(0, 16, spreading, 0, unroll=8)
    gives = jnp.dot(to_slots, values[...].astype(BF), preferred_element_type=F32).astype(BF)
    giving[...] = gives.reshape(16, 16, 256)
    for q in FAR:
        give_copy(q).start()
    given[0] = giving[0]

    def place(q):
        row, _ = spots(q)
        mask = rows_of == row
        amount = given[q].astype(F32)
        rows = []
        for i in range(3):
            line = jnp.concatenate([amount[4 * c + i : 4 * c + i + 1] for c in range(CAP)], axis=1)
            rows.append(jnp.where(mask, line, 0.0).astype(BF))
        return lax.dot_general(jnp.concatenate(rows, axis=0), hots[q], NT, preferred_element_type=F32)

    adding[...] = place(0)

    def place_far(turn, carry):
        total = None
        for c in range(5):
            q = ordered(NEAR, turn, c)
            give_arrival(q).wait_recv()
            piece = place(q)
            total = piece if total is None else total + piece
        adding[...] += total
        return carry

    lax.fori_loop(0, 3, place_far, 0)
    for i in range(3):
        part[i] = adding[128 * i : 128 * i + 128, :].reshape(8, 16, 256).astype(BF)

    def part_copy(by):
        return pltpu.make_async_remote_copy(
            src_ref=part.at[:, group_at(by)],
            dst_ref=got.at[11 + groups - by],
            send_sem=part_send.at[by],
            recv_sem=part_recv.at[groups - by],
            device_id=(slab, group_at(by)),
            device_id_type=MESH,
        )

    def part_arrival(by):
        return pltpu.make_async_remote_copy(
            src_ref=part.at[:, group_at(by)],
            dst_ref=got.at[11 + by],
            send_sem=part_send.at[by],
            recv_sem=part_recv.at[by],
            device_id=(slab, group_at(by)),
            device_id_type=MESH,
        )

    for by in (4, 3, 5, 2, 6, 1, 7):
        part_copy(by).start()
    share = part[:, group].astype(F32)
    for by in (1, 7, 2, 6, 3, 5, 4):
        part_arrival(by).wait_recv()
        share = share + got[11 + by].astype(F32)
    halves[:, group] = share.astype(BF)
    half_begin()
    half_finish()
    for i in range(3):
        out[i] = state[i] + halves[i].reshape(128, 256).astype(F32)

    def end_far(q, carry):
        ask_copy(q).wait_send()
        ans_copy(q).wait_send()
        give_copy(q).wait_send()
        return carry

    pl.when(has_above)(to_above.wait_send)
    pl.when(has_below)(to_below.wait_send)
    for side in range(3):
        pair_copy(side).wait_send()
    def sent(first, last):
        for k in range(first, last):
            force_copy(k).wait_send()

    pl.when(has_below)(lambda: sent(0, 4))
    pl.when(has_above)(lambda: sent(4, 8))
    sent(8, 11)
    lax.fori_loop(1, 16, end_far, 0)
    sum_close()
    for by in range(1, groups):
        part_copy(by).wait_send()
    half_close()


def body(
    disp_now, disp_prev, inv_mass, cell_nodes, shape_grads, cell_weights, cell_shear, cell_bulk,
    block_owner, block_nodes, block_phi, block_corr, block_target, block_fixed,
):
    vmem = pl.BlockSpec(memory_space=pltpu.VMEM)
    anywhere = pl.BlockSpec(memory_space=pl.ANY)
    dma = pltpu.SemaphoreType.DMA
    message = pltpu.VMEM((16, 16, 256), BF)
    nodal = pltpu.VMEM((3, 8, 16, 256), BF)
    paired = pltpu.VMEM((3, 3, 4, 16, 256), BF)
    result = pl.pallas_call(
        step_kernel,
        name="step",
        out_shape=jax.ShapeDtypeStruct((3, 128, 256), F32),
        in_specs=[anywhere] * 3 + [vmem, anywhere] + [vmem] * 5 + [anywhere] * 2 + [vmem] * 2,
        out_specs=vmem,
        scratch_shapes=[
            pltpu.VMEM((3, 32768), F32),
            pltpu.VMEM((3, 32768), F32),
            pltpu.VMEM((256, 128), F32),
            pltpu.VMEM((3, 128, 256), F32),
            pltpu.VMEM((3, 384, 256), BF),
            pltpu.VMEM((8, 1, QUAD), jnp.int32),
            pltpu.VMEM((32, 3, 192, 128), BF),
            pltpu.VMEM((3, 128, 128), F32),
            pltpu.VMEM((8, 8, QUAD), F32),
            pltpu.VMEM((8, 3, 256, QUAD), BF),
            pltpu.VMEM((8, 384, QUAD), BF),
            pltpu.VMEM((3, 3, 4, 2, 16, 256), BF),
            paired,
            paired,
            pltpu.VMEM((3, 16, 256), F32),
            pltpu.VMEM((19, 3, 16, 256), BF),
            nodal,
            message, message, message, message, message, message,
            pltpu.VMEM((384, 256), F32),
            nodal,
            nodal,
            pltpu.VMEM((16, 256, 256), F32),
            pltpu.VMEM((16, 256, 128), F32),
            pltpu.VMEM((16, 256, 256), BF),
            pltpu.VMEM((16, 256, 128), BF),
            pltpu.VMEM((128, 128), F32),
            pltpu.VMEM((128, 128), F32),
            pltpu.VMEM((2, 128, 128), F32),
            pltpu.VMEM((128, 256), F32),
            pltpu.VMEM((128, 128), F32),
            pltpu.VMEM((384, 256), BF),
            pltpu.VMEM((16, 256, 1024), BF),
            dma((6,)), pltpu.SemaphoreType.REGULAR, dma((3,)), dma((3,)), dma((3,)), dma((3,)), dma((11,)), dma((11,)),
            dma((8,)), dma((8,)), dma((16,)), dma((16,)), dma((16,)), dma((16,)), dma((16,)), dma((16,)), dma((8,)),
            dma((8,)), dma((8,)), dma((8,)),
        ],
        compiler_params=pltpu.CompilerParams(
            vmem_limit_bytes=60 << 20, collective_id=0, has_side_effects=True
        ),
    )(
        disp_now,
        disp_prev,
        inv_mass.reshape(256, 128),
        cell_nodes,
        shape_grads,
        cell_weights,
        cell_shear.reshape(1, 32),
        cell_bulk.reshape(1, 32),
        block_owner.reshape(1, 32),
        block_nodes,
        block_phi.reshape(16, 256, 256),
        block_corr.reshape(16, 256, 128),
        jnp.moveaxis(block_target, 1, 0),
        block_fixed,
    )
    return result.reshape(3, 32768)


def solution(mesh):
    both = ("slab", "group")
    placed = (
        P(None, "slab"), P(None, "slab"), P("slab"), P(both, None), P(both, None, None, None), P(both, None),
        P(both), P(both), P(both, None), P(both, None), P(both, None, None), P(both, None, None),
        P(both, None, None), P(both, None),
    )
    return jax.shard_map(body, mesh=mesh, in_specs=placed, out_specs=P(None, "slab"), check_vma=False)
```

```python
import jax
import jax.numpy as jnp
from jax import lax
from jax.experimental import pallas as pl
from jax.experimental.pallas import tpu as pltpu
from jax.sharding import PartitionSpec as P

BF = jnp.bfloat16
F32 = jnp.float32
NT = (((1,), (1,)), ((), ()))
MESH = pl.DeviceIdType.MESH
CAP = 4
QUAD = 768
FAR = tuple(range(1, 16))
NEAR = FAR


def onehot(index, size):
    rows = lax.broadcasted_iota(jnp.int32, (size, index.shape[1]), 0)
    return jnp.where(rows == index, 1.0, 0.0).astype(BF)


def step_kernel(
    now_hbm, prev_hbm, mass_hbm, cell_nodes_hbm, grads_hbm, weights_hbm, shear_hbm, bulk_hbm, owner_hbm, block_nodes_hbm,
    phi_hbm, corr_hbm, target_hbm, fixed_hbm, out,
    cell_nodes, weights, shear, bulk, owner, block_nodes, target, fixed,
    lines, prev, mass, state, tables, nodes, grads, field, near, columns, spread, forces, paired, merged, pooled,
    got, summed, asking, asked, answer, answered, giving, given, adding, part, halves,
    phi, corr, phi_bf, corr_bf, goal, held, numbers, values, resids, gathered, hots,
    load_sem, enter_sem, pair_send, pair_recv, halo_send, halo_recv, force_send, force_recv, all_send, all_recv, ask_send, ask_recv, ans_send, ans_recv,
    give_send, give_recv, part_send, part_recv, half_send, half_recv,
):
    slab, group = lax.axis_index("slab"), lax.axis_index("group")
    slabs, groups = 16, 8

    def slab_at(by):
        return lax.rem(slab + by + slabs, slabs)

    depth, core = group // 2, lax.rem(group, 2)
    depths = groups // 2
    sibling = (slab, depth * 2 + 1 - core)

    def depth_at(by):
        return lax.rem(depth + by, depths)

    def level(by):
        return depth_at(by) * 2 + core

    def group_at(by):
        return lax.rem(group + by, groups)

    load_now = pltpu.make_async_copy(now_hbm, lines, load_sem.at[0])
    load_grads = pltpu.make_async_copy(grads_hbm, grads, load_sem.at[1])
    load_prev = pltpu.make_async_copy(prev_hbm, prev, load_sem.at[2])
    load_mass = pltpu.make_async_copy(mass_hbm, mass, load_sem.at[3])
    load_phi = pltpu.make_async_copy(phi_hbm, phi, load_sem.at[4])
    load_corr = pltpu.make_async_copy(corr_hbm, corr, load_sem.at[5])
    small = [
        pltpu.make_async_copy(source, place, load_sem.at[6 + k])
        for k, (source, place) in enumerate(
            (
                (owner_hbm, owner), (block_nodes_hbm, block_nodes), (cell_nodes_hbm, cell_nodes),
                (weights_hbm, weights), (shear_hbm, shear), (bulk_hbm, bulk), (target_hbm, target), (fixed_hbm, fixed),
            )
        )
    ]
    load_now.start()
    for load in small:
        load.start()
    load_grads.start()
    load_prev.start()
    load_mass.start()
    load_phi.start()
    load_corr.start()

    barrier = pltpu.get_barrier_semaphore()

    def greet(device):
        pl.semaphore_signal(barrier, inc=1, device_id=device, device_id_type=MESH)

    def greet_again(device):
        pl.semaphore_signal(enter_sem, inc=1, device_id=device, device_id_type=MESH)

    for by in (1, 15, 4, 8, 12, 6, 10):
        greet((slab_at(by), group))
    for by in (1, 2, 3):
        greet((slab, level(by)))
    greet(sibling)

    def relaid(source, use):
        def move(block, carry):
            start = pl.multiple_of(block * 2048, 2048)
            wide = source[:, pl.ds(start, 2048)]
            at = pl.ds(pl.multiple_of(block * 8, 8), 8)
            for i in range(3):
                use(i, at, jnp.concatenate([wide[i : i + 1, 256 * r : 256 * r + 256] for r in range(8)], axis=0))
            return carry

        lax.fori_loop(0, 16, move, 0, unroll=4)

    def set_state(i, at, value):
        state[i, at, :] = value

    load_now.wait()
    for load in small:
        load.wait()
    relaid(lines, set_state)
    for i in range(3):
        tables[1, 128 * i : 128 * i + 128, :] = state[i].astype(BF)
    pl.semaphore_wait(barrier, 11)

    def halo(side, by):
        return pltpu.make_async_remote_copy(
            src_ref=tables.at[1],
            dst_ref=tables.at[side],
            send_sem=halo_send.at[side],
            recv_sem=halo_recv.at[side],
            device_id=(slab_at(by), group),
            device_id_type=MESH,
        )

    to_above, to_below = halo(0, 1), halo(2, -1)
    has_below, has_above = slab > 0, slab < slabs - 1
    pl.when(has_above)(to_above.start)
    pl.when(has_below)(to_below.start)
    for by in (1, 15):
        greet_again((slab_at(by), group))
    for by in (1, 2, 3):
        greet_again((slab, level(by)))

    own_row = owner[...]
    diag = lax.broadcasted_iota(jnp.int32, (32, 32), 0) == lax.broadcasted_iota(jnp.int32, (32, 32), 1)
    own_col = jnp.sum(jnp.where(diag, own_row, 0), axis=1, keepdims=True)
    block_wide = lax.broadcasted_iota(jnp.int32, (32, 128), 0)
    of_lane = lax.broadcasted_iota(jnp.int32, (32, 128), 1) // 4
    own_wide = jnp.sum(jnp.where(block_wide == of_lane, own_col, 0), axis=0, keepdims=True)
    earlier = (own_col == own_wide) & (block_wide < of_lane)
    rank = jnp.sum(jnp.where(earlier, 1, 0), axis=0, keepdims=True)
    relative = own_wide - slab
    relative = jnp.where(relative < 0, relative + slabs, relative)
    key = relative * 16 + rank * 4 + lax.broadcasted_iota(jnp.int32, (1, 128), 1) % 4
    to_slots = onehot(key, 256)
    square = lax.broadcasted_iota(jnp.int32, (128, 128), 0) == lax.broadcasted_iota(jnp.int32, (128, 128), 1)
    key_col = jnp.sum(jnp.where(square, key, 0), axis=1, keepdims=True)

    node = block_nodes[...]
    numbers[...] = jnp.zeros_like(numbers)
    for side in range(2):
        span = slice(128 * side, 128 * side + 128)
        numbers[side, pl.ds(0, 32, stride=4), :] = ((node[:, span] >> 8) + 1).astype(F32)
        numbers[side, pl.ds(1, 32, stride=4), :] = ((node[:, span] & 255) + 1).astype(F32)
    named = jnp.concatenate([numbers[0], numbers[1]], axis=1).astype(BF)
    asks = jnp.dot(to_slots, named, preferred_element_type=F32) - 1.0
    asking[...] = asks.astype(BF).reshape(16, 16, 256)

    def exchange(source, landing, send, recv):
        def copy(q):
            return pltpu.make_async_remote_copy(
                src_ref=source.at[q],
                dst_ref=landing.at[slabs - q],
                send_sem=send.at[q],
                recv_sem=recv.at[slabs - q],
                device_id=(slab_at(q), group),
                device_id_type=MESH,
            )

        def arrival(q):
            return pltpu.make_async_remote_copy(
                src_ref=source.at[q],
                dst_ref=landing.at[q],
                send_sem=send.at[q],
                recv_sem=recv.at[q],
                device_id=(slab_at(q), group),
                device_id_type=MESH,
            )

        return copy, arrival

    def ordered(order, turn, c):
        q = order[c]
        for t in range(1, 3):
            q = jnp.where(turn == t, order[5 * t + c], q)
        return q

    ask_copy, ask_arrival = exchange(asking, asked, ask_send, ask_recv)
    ans_copy, ans_arrival = exchange(answer, answered, ans_send, ans_recv)
    give_copy, give_arrival = exchange(giving, given, give_send, give_recv)

    pl.semaphore_wait(enter_sem, 5)
    for q in FAR:
        ask_copy(q).start()
    asked[0] = asking[0]

    def flatten(quad, carry):
        rows = [cell_nodes[pl.ds(4 * quad + e, 1), :] for e in range(4)]
        nodes[quad] = jnp.concatenate(rows, axis=1)
        return carry

    lax.fori_loop(0, 8, flatten, 0, unroll=4)
    rows_quad = lax.broadcasted_iota(jnp.int32, (128, QUAD), 0)

    def pick(total, row):
        mask = rows_quad == row
        return [
            jnp.sum(jnp.where(mask, total[128 * i : 128 * i + 128], 0.0), axis=0, keepdims=True) for i in range(3)
        ]

    def gather_own(quad, carry):
        number = nodes[quad]
        side_of, row, column = number >> 15, (number >> 8) & 127, number & 255
        for side in range(3):
            columns[quad, side] = onehot(jnp.where(side_of == side, column, -1), 256)
        total = jnp.dot(tables[1], columns[quad, 1], preferred_element_type=F32)
        for i, line in enumerate(pick(total, row)):
            near[quad, i : i + 1, :] = line
        return carry

    lax.fori_loop(0, 8, gather_own, 0, unroll=2)
    load_prev.wait()

    def set_base(i, at, value):
        state[i, at, :] = 2.0 * state[i, at, :] - value

    relaid(prev, set_base)
    def absent(side):
        tables[side] = jnp.zeros((384, 256), BF)

    pl.when(has_below)(to_above.wait_recv)
    pl.when(has_above)(to_below.wait_recv)
    pl.when(slab == 0)(lambda: absent(0))
    pl.when(slab == slabs - 1)(lambda: absent(2))

    def gather_sides(quad, carry):
        row = (nodes[quad] >> 8) & 127
        total = jnp.dot(tables[0], columns[quad, 0], preferred_element_type=F32)
        total += jnp.dot(tables[2], columns[quad, 2], preferred_element_type=F32)
        for i, line in enumerate(pick(total, row)):
            near[quad, i : i + 1, :] += line
        return carry

    lax.fori_loop(0, 8, gather_sides, 0, unroll=4)
    load_grads.wait()
    sub = lax.broadcasted_iota(jnp.int32, (8, 384), 0)
    lane = lax.broadcasted_iota(jnp.int32, (8, 384), 1)
    own = (sub >= 4) == (lane >= 192)

    def gradient(quad, carry):
        for pair in range(2):
            left = jnp.zeros((8, 384), F32)
            for i in range(3):
                left = jnp.where(sub % 4 == i, near[quad, i : i + 1, 384 * pair : 384 * pair + 384], left)
            left = jnp.where(own, left, 0.0).astype(BF)
            for j in range(3):
                first = 4 * quad + 2 * pair
                both = jnp.concatenate([grads[first, j], grads[first + 1, j]], axis=0)
                at = pl.ds(pl.multiple_of(16 * quad + 8 * pair, 8), 8)
                field[j, at, :] = jnp.dot(left, both, preferred_element_type=F32)
        return carry

    lax.fori_loop(0, 8, gradient, 0, unroll=8)
    full = [
        [field[j, pl.ds(i, 32, stride=4), :] + (1.0 if i == j else 0.0) for j in range(3)]
        for i in range(3)
    ]
    cofactor = [
        [
            full[(i + 1) % 3][(j + 1) % 3] * full[(i + 2) % 3][(j + 2) % 3]
            - full[(i + 1) % 3][(j + 2) % 3] * full[(i + 2) % 3][(j + 1) % 3]
            for j in range(3)
        ]
        for i in range(3)
    ]
    volume = full[0][0] * cofactor[0][0] + full[0][1] * cofactor[0][1] + full[0][2] * cofactor[0][2]
    clamped = jnp.maximum(volume, 0.3)
    mu = jnp.sum(jnp.where(diag, shear[...], 0.0), axis=1, keepdims=True)
    lam = jnp.sum(jnp.where(diag, bulk[...], 0.0), axis=1, keepdims=True)
    weight = weights[...]
    factor = (lam * jnp.log(clamped) - mu) / clamped
    for i in range(3):
        for j in range(3):
            field[j, pl.ds(i, 32, stride=4), :] = weight * (mu * full[i][j] + factor * cofactor[i][j])
    low_lane = lax.broadcasted_iota(jnp.int32, (1, 384), 1) < 192
    rows_pair = lax.broadcasted_iota(jnp.int32, (128, 384), 0)

    def cell_forces(quad, carry):
        for pair in range(2):
            total = None
            for j in range(3):
                first = 4 * quad + 2 * pair
                at = pl.ds(pl.multiple_of(16 * quad + 8 * pair, 8), 8)
                both = jnp.concatenate([grads[first, j], grads[first + 1, j]], axis=0)
                piece = lax.dot_general(field[j, at, :].astype(BF), both, NT, preferred_element_type=F32)
                total = piece if total is None else total + piece
            span = slice(384 * pair, 384 * pair + 384)
            mask = rows_pair == ((nodes[quad, :, span] >> 8) & 127)
            for i in range(3):
                value = jnp.where(low_lane, total[i : i + 1], total[4 + i : 5 + i])
                spread[quad, 128 * i : 128 * i + 128, span] = jnp.where(mask, value, 0.0).astype(BF)
        return carry

    lax.fori_loop(0, 8, cell_forces, 0, unroll=8)

    def pair_copy(side):
        return pltpu.make_async_remote_copy(
            src_ref=forces.at[side, :, :, 1 - core],
            dst_ref=paired.at[side],
            send_sem=pair_send.at[side],
            recv_sem=pair_recv.at[side],
            device_id=sibling,
            device_id_type=MESH,
        )

    def force_copy(k):
        source, shift, by = ((0, -1, k), (2, 1, k - 4), (1, 0, k - 7))[k // 4]
        return pltpu.make_async_remote_copy(
            src_ref=merged.at[source, :, depth_at(by)],
            dst_ref=got.at[k],
            send_sem=force_send.at[k],
            recv_sem=force_recv.at[k],
            device_id=(slab_at(shift), level(by)),
            device_id_type=MESH,
        )

    def scatter(side):
        total = None
        for quad in range(8):
            piece = lax.dot_general(spread[quad], columns[quad, side], NT, preferred_element_type=F32)
            total = piece if total is None else total + piece
        for i in range(3):
            forces[side, i] = total[128 * i : 128 * i + 128].reshape(4, 2, 16, 256).astype(BF)
        pair_copy(side).start()

    def merge(side, first, last):
        pair_copy(side).wait_recv()
        for i in range(3):
            merged[side, i] = (forces[side, i, :, core].astype(F32) + paired[side, i].astype(F32)).astype(BF)
        def leave():
            for k in range(first, last):
                force_copy(k).start()

        pl.when((has_below, slab >= 0, has_above)[side])(leave)

    scatter(0)
    scatter(2)
    merge(0, 0, 4)
    scatter(1)
    merge(2, 4, 8)

    def spots(q):
        spot = asked[q].astype(F32)
        row = jnp.concatenate([spot[4 * c : 4 * c + 1] for c in range(CAP)], axis=1).astype(jnp.int32)
        column = jnp.concatenate([spot[4 * c + 1 : 4 * c + 2] for c in range(CAP)], axis=1).astype(jnp.int32)
        return row, column

    def heat(q):
        hots[q] = onehot(spots(q)[1], 256)

    def heat_far(q, carry):
        ask_arrival(q).wait_recv()
        heat(q)
        return carry

    heat(0)
    merge(1, 8, 11)
    lax.fori_loop(1, 16, heat_far, 0, unroll=3)
    for i in range(3):
        goal[pl.ds(i, 32, stride=4), :] = target[i]
    goal[pl.ds(3, 32, stride=4), :] = jnp.zeros((32, 128), F32)
    for i in range(4):
        held[pl.ds(i, 32, stride=4), :] = fixed[...].astype(F32)
    load_phi.wait()
    load_corr.wait()

    def narrow(pair, carry):
        phi_bf[pair] = phi[pair].astype(BF)
        corr_bf[pair] = corr[pair].astype(BF)
        return carry

    lax.fori_loop(0, 16, narrow, 0)
    load_mass.wait()

    pooled[...] = merged[1, :, depth].astype(F32)

    def collect(first, last):
        value = pooled[...]
        for k in range(first, last):
            force_copy(k).wait_recv()
            value = value + got[k].astype(F32)
        pooled[...] = value

    collect(8, 11)
    pl.when(has_above)(lambda: collect(0, 4))
    pl.when(has_below)(lambda: collect(4, 8))

    def shared(buffer, send, recv):
        def copy(by):
            return pltpu.make_async_remote_copy(
                src_ref=buffer.at[:, group],
                dst_ref=buffer.at[:, group],
                send_sem=send.at[by],
                recv_sem=recv.at[groups - by],
                device_id=(slab, group_at(by)),
                device_id_type=MESH,
            )

        def arrival(by):
            return pltpu.make_async_remote_copy(
                src_ref=buffer.at[:, group_at(by)],
                dst_ref=buffer.at[:, group_at(by)],
                send_sem=send.at[by],
                recv_sem=recv.at[by],
                device_id=(slab, group_at(by)),
                device_id_type=MESH,
            )

        def begin():
            for by in (4, 3, 5, 2, 6, 1, 7):
                copy(by).start()

        def finish():
            for by in (1, 7, 2, 6, 3, 5, 4):
                arrival(by).wait_recv()

        def close():
            for by in range(1, groups):
                copy(by).wait_send()

        return begin, finish, close

    sum_begin, sum_finish, sum_close = shared(summed, all_send, all_recv)
    half_begin, half_finish, half_close = shared(halves, half_send, half_recv)
    summed[:, group] = pooled[...].astype(BF)
    sum_begin()
    scale = jnp.concatenate([mass[pl.ds(0, 128, stride=2), :], mass[pl.ds(1, 128, stride=2), :]], axis=1)
    sum_finish()
    for i in range(3):
        state[i] = state[i] - scale * summed[i].reshape(128, 256).astype(F32)
        gathered[128 * i : 128 * i + 128, :] = state[i].astype(BF)

    rows_of = lax.broadcasted_iota(jnp.int32, (128, 1024), 0)
    sixteen = lax.broadcasted_iota(jnp.int32, (16, 256), 0)

    def look(q):
        row, _ = spots(q)
        hit = jnp.dot(gathered[...], hots[q], preferred_element_type=F32)
        mask = rows_of == row
        found = jnp.zeros((16, 256), F32)
        for i in range(3):
            line = jnp.sum(jnp.where(mask, hit[128 * i : 128 * i + 128], 0.0), axis=0, keepdims=True)
            for c in range(CAP):
                found = jnp.where(sixteen == 4 * c + i, line[:, 256 * c : 256 * c + 256], found)
        return found.astype(BF)

    def look_far(turn, carry):
        for c in range(5):
            q = ordered(FAR, turn, c)
            answer[q] = look(q)
            ans_copy(q).start()
        return carry

    lax.fori_loop(0, 3, look_far, 0)
    answered[0] = look(0)
    to_blocks = jnp.where(lax.broadcasted_iota(jnp.int32, (128, 256), 1) == key_col, 1.0, 0.0).astype(BF)

    for q in NEAR:
        ans_arrival(q).wait_recv()
    values[...] = jnp.dot(to_blocks, answered[...].reshape(256, 256), preferred_element_type=F32)

    upper = lax.broadcasted_iota(jnp.int32, (8, 128), 0) < 4

    def at_pair(pair):
        return pl.ds(pl.multiple_of(8 * pair, 8), 8)

    def residual(pair, carry):
        at = at_pair(pair)
        both = lax.dot_general(values[at, :].astype(BF), phi_bf[pair], NT, preferred_element_type=F32)
        interp = jnp.where(upper, both[:, :128], both[:, 128:])
        resids[at, :] = held[at, :] * (goal[at, :] - interp)
        return carry

    def correction(pair, carry):
        at = at_pair(pair)
        both = lax.dot_general(resids[at, :].astype(BF), corr_bf[pair], NT, preferred_element_type=F32)
        values[at, 0:128] = jnp.where(upper, both[:, :128], 0.0)
        values[at, 128:256] = jnp.where(upper, 0.0, both[:, 128:])
        return carry

    def spreading(pair, carry):
        at = at_pair(pair)
        values[at, :] = jnp.dot(values[at, :].astype(BF), phi_bf[pair], preferred_element_type=F32)
        return carry

    lax.fori_loop(0, 16, residual, 0, unroll=16)
    lax.fori_loop(0, 16, correction, 0, unroll=16)
    lax.fori_loop(0, 16, spreading, 0, unroll=16)
    gives = jnp.dot(to_slots, values[...].astype(BF), preferred_element_type=F32).astype(BF)
    giving[...] = gives.reshape(16, 16, 256)
    for q in FAR:
        give_copy(q).start()
    given[0] = giving[0]

    def place(q):
        row, _ = spots(q)
        mask = rows_of == row
        amount = given[q].astype(F32)
        rows = []
        for i in range(3):
            line = jnp.concatenate([amount[4 * c + i : 4 * c + i + 1] for c in range(CAP)], axis=1)
            rows.append(jnp.where(mask, line, 0.0).astype(BF))
        return lax.dot_general(jnp.concatenate(rows, axis=0), hots[q], NT, preferred_element_type=F32)

    adding[...] = place(0)

    def place_far(turn, carry):
        total = None
        for c in range(5):
            q = ordered(NEAR, turn, c)
            give_arrival(q).wait_recv()
            piece = place(q)
            total = piece if total is None else total + piece
        adding[...] += total
        return carry

    lax.fori_loop(0, 3, place_far, 0)
    for i in range(3):
        part[i] = adding[128 * i : 128 * i + 128, :].reshape(8, 16, 256).astype(BF)

    def part_copy(by):
        return pltpu.make_async_remote_copy(
            src_ref=part.at[:, group_at(by)],
            dst_ref=got.at[11 + groups - by],
            send_sem=part_send.at[by],
            recv_sem=part_recv.at[groups - by],
            device_id=(slab, group_at(by)),
            device_id_type=MESH,
        )

    def part_arrival(by):
        return pltpu.make_async_remote_copy(
            src_ref=part.at[:, group_at(by)],
            dst_ref=got.at[11 + by],
            send_sem=part_send.at[by],
            recv_sem=part_recv.at[by],
            device_id=(slab, group_at(by)),
            device_id_type=MESH,
        )

    for by in (4, 3, 5, 2, 6, 1, 7):
        part_copy(by).start()
    share = part[:, group].astype(F32)
    for by in (1, 7, 2, 6, 3, 5, 4):
        part_arrival(by).wait_recv()
        share = share + got[11 + by].astype(F32)
    halves[:, group] = share.astype(BF)
    half_begin()
    half_finish()
    for i in range(3):
        out[i] = state[i] + halves[i].reshape(128, 256).astype(F32)

    def end_far(q, carry):
        ask_copy(q).wait_send()
        ans_copy(q).wait_send()
        give_copy(q).wait_send()
        return carry

    pl.when(has_above)(to_above.wait_send)
    pl.when(has_below)(to_below.wait_send)
    for side in range(3):
        pair_copy(side).wait_send()
    def sent(first, last):
        for k in range(first, last):
            force_copy(k).wait_send()

    pl.when(has_below)(lambda: sent(0, 4))
    pl.when(has_above)(lambda: sent(4, 8))
    sent(8, 11)
    lax.fori_loop(1, 16, end_far, 0)
    sum_close()
    for by in range(1, groups):
        part_copy(by).wait_send()
    half_close()


def body(
    disp_now, disp_prev, inv_mass, cell_nodes, shape_grads, cell_weights, cell_shear, cell_bulk,
    block_owner, block_nodes, block_phi, block_corr, block_target, block_fixed,
):
    vmem = pl.BlockSpec(memory_space=pltpu.VMEM)
    hbm = pl.BlockSpec(memory_space=pltpu.HBM)
    dma = pltpu.SemaphoreType.DMA
    message = pltpu.VMEM((16, 16, 256), BF)
    nodal = pltpu.VMEM((3, 8, 16, 256), BF)
    paired = pltpu.VMEM((3, 3, 4, 16, 256), BF)
    result = pl.pallas_call(
        step_kernel,
        name="step",
        out_shape=jax.ShapeDtypeStruct((3, 128, 256), F32),
        in_specs=[hbm] * 14,
        out_specs=vmem,
        scratch_shapes=[
            pltpu.VMEM((32, 192), jnp.int32),
            pltpu.VMEM((32, 128), F32),
            pltpu.VMEM((1, 32), F32),
            pltpu.VMEM((1, 32), F32),
            pltpu.VMEM((1, 32), jnp.int32),
            pltpu.VMEM((32, 256), jnp.int32),
            pltpu.VMEM((3, 32, 128), F32),
            pltpu.VMEM((32, 128), jnp.int32),
            pltpu.VMEM((3, 32768), F32),
            pltpu.VMEM((3, 32768), F32),
            pltpu.VMEM((256, 128), F32),
            pltpu.VMEM((3, 128, 256), F32),
            pltpu.VMEM((3, 384, 256), BF),
            pltpu.VMEM((8, 1, QUAD), jnp.int32),
            pltpu.VMEM((32, 3, 192, 128), BF),
            pltpu.VMEM((3, 128, 128), F32),
            pltpu.VMEM((8, 8, QUAD), F32),
            pltpu.VMEM((8, 3, 256, QUAD), BF),
            pltpu.VMEM((8, 384, QUAD), BF),
            pltpu.VMEM((3, 3, 4, 2, 16, 256), BF),
            paired,
            paired,
            pltpu.VMEM((3, 16, 256), F32),
            pltpu.VMEM((19, 3, 16, 256), BF),
            nodal,
            message, message, message, message, message, message,
            pltpu.VMEM((384, 256), F32),
            nodal,
            nodal,
            pltpu.VMEM((16, 256, 256), F32),
            pltpu.VMEM((16, 256, 128), F32),
            pltpu.VMEM((16, 256, 256), BF),
            pltpu.VMEM((16, 256, 128), BF),
            pltpu.VMEM((128, 128), F32),
            pltpu.VMEM((128, 128), F32),
            pltpu.VMEM((2, 128, 128), F32),
            pltpu.VMEM((128, 256), F32),
            pltpu.VMEM((128, 128), F32),
            pltpu.VMEM((384, 256), BF),
            pltpu.VMEM((16, 256, 1024), BF),
            dma((14,)), pltpu.SemaphoreType.REGULAR, dma((3,)), dma((3,)), dma((3,)), dma((3,)), dma((11,)), dma((11,)),
            dma((8,)), dma((8,)), dma((16,)), dma((16,)), dma((16,)), dma((16,)), dma((16,)), dma((16,)), dma((8,)),
            dma((8,)), dma((8,)), dma((8,)),
        ],
        compiler_params=pltpu.CompilerParams(
            vmem_limit_bytes=60 << 20, collective_id=0, has_side_effects=True
        ),
    )(
        disp_now,
        disp_prev,
        inv_mass.reshape(256, 128),
        cell_nodes,
        shape_grads,
        cell_weights,
        cell_shear.reshape(1, 32),
        cell_bulk.reshape(1, 32),
        block_owner.reshape(1, 32),
        block_nodes,
        block_phi.reshape(16, 256, 256),
        block_corr.reshape(16, 256, 128),
        jnp.moveaxis(block_target, 1, 0),
        block_fixed,
    )
    return result.reshape(3, 32768)


def solution(mesh):
    both = ("slab", "group")
    placed = (
        P(None, "slab"), P(None, "slab"), P("slab"), P(both, None), P(both, None, None, None), P(both, None),
        P(both), P(both), P(both, None), P(both, None), P(both, None, None), P(both, None, None),
        P(both, None, None), P(both, None),
    )
    return jax.shard_map(body, mesh=mesh, in_specs=placed, out_specs=P(None, "slab"), check_vma=False)
```

```python
import jax
import jax.numpy as jnp
from jax import lax
from jax.experimental import pallas as pl
from jax.experimental.pallas import tpu as pltpu
from jax.sharding import PartitionSpec as P

BF = jnp.bfloat16
F32 = jnp.float32
NT = (((1,), (1,)), ((), ()))
MESH = pl.DeviceIdType.MESH
CAP = 4
QUAD = 768
FAR = tuple(range(1, 16))
NEAR = FAR


def onehot(index, size):
    rows = lax.broadcasted_iota(jnp.int32, (size, index.shape[1]), 0)
    return jnp.where(rows == index, 1.0, 0.0).astype(BF)


def step_kernel(
    now_hbm, prev_hbm, mass_hbm, cell_nodes_hbm, grads_hbm, weights_hbm, shear_hbm, bulk_hbm, owner_hbm, block_nodes_hbm,
    phi_hbm, corr_hbm, target_hbm, fixed_hbm, out,
    cell_nodes, weights, shear, bulk, owner, block_nodes, target, fixed,
    lines, prev, mass, state, tables, nodes, grads, field, near, columns, spread, forces, paired, merged, pooled,
    got, summed, asking, asked, answer, answered, giving, given, adding, part, halves,
    phi, corr, phi_bf, corr_bf, goal, held, numbers, values, resids, gathered, hots,
    load_sem, enter_sem, pair_send, pair_recv, halo_send, halo_recv, force_send, force_recv, all_send, all_recv, ask_send, ask_recv, ans_send, ans_recv,
    give_send, give_recv, part_send, part_recv, half_send, half_recv,
):
    slab, group = lax.axis_index("slab"), lax.axis_index("group")
    slabs, groups = 16, 8

    def slab_at(by):
        return lax.rem(slab + by + slabs, slabs)

    depth, core = group // 2, lax.rem(group, 2)
    depths = groups // 2
    sibling = (slab, depth * 2 + 1 - core)

    def depth_at(by):
        return lax.rem(depth + by, depths)

    def level(by):
        return depth_at(by) * 2 + core

    def group_at(by):
        return lax.rem(group + by, groups)

    load_now = pltpu.make_async_copy(now_hbm, lines, load_sem.at[0])
    load_grads = pltpu.make_async_copy(grads_hbm, grads, load_sem.at[1])
    load_prev = pltpu.make_async_copy(prev_hbm, prev, load_sem.at[2])
    load_mass = pltpu.make_async_copy(mass_hbm, mass, load_sem.at[3])
    load_phi = pltpu.make_async_copy(phi_hbm, phi, load_sem.at[4])
    load_corr = pltpu.make_async_copy(corr_hbm, corr, load_sem.at[5])
    small = [
        pltpu.make_async_copy(source, place, load_sem.at[6 + k])
        for k, (source, place) in enumerate(
            (
                (owner_hbm, owner), (block_nodes_hbm, block_nodes), (cell_nodes_hbm, cell_nodes),
                (weights_hbm, weights), (shear_hbm, shear), (bulk_hbm, bulk), (target_hbm, target), (fixed_hbm, fixed),
            )
        )
    ]
    load_now.start()
    for load in small:
        load.start()
    load_grads.start()
    load_prev.start()
    load_mass.start()
    load_phi.start()
    load_corr.start()

    barrier = pltpu.get_barrier_semaphore()

    def greet(device):
        pl.semaphore_signal(barrier, inc=1, device_id=device, device_id_type=MESH)

    def greet_again(device):
        pl.semaphore_signal(enter_sem, inc=1, device_id=device, device_id_type=MESH)

    for by in (1, 15, 4, 8, 12, 6, 10):
        greet((slab_at(by), group))
    for by in (1, 2, 3):
        greet((slab, level(by)))
    greet(sibling)

    def relaid(source, use):
        def move(block, carry):
            start = pl.multiple_of(block * 2048, 2048)
            wide = source[:, pl.ds(start, 2048)]
            at = pl.ds(pl.multiple_of(block * 8, 8), 8)
            for i in range(3):
                use(i, at, jnp.concatenate([wide[i : i + 1, 256 * r : 256 * r + 256] for r in range(8)], axis=0))
            return carry

        lax.fori_loop(0, 16, move, 0, unroll=4)

    def set_state(i, at, value):
        state[i, at, :] = value

    load_now.wait()
    for load in small:
        load.wait()
    relaid(lines, set_state)
    for i in range(3):
        tables[1, 128 * i : 128 * i + 128, :] = state[i].astype(BF)
    pl.semaphore_wait(barrier, 11)

    def halo(side, by):
        return pltpu.make_async_remote_copy(
            src_ref=tables.at[1],
            dst_ref=tables.at[side],
            send_sem=halo_send.at[side],
            recv_sem=halo_recv.at[side],
            device_id=(slab_at(by), group),
            device_id_type=MESH,
        )

    to_above, to_below = halo(0, 1), halo(2, -1)
    has_below, has_above = slab > 0, slab < slabs - 1
    pl.when(has_above)(to_above.start)
    pl.when(has_below)(to_below.start)
    for by in (1, 15):
        greet_again((slab_at(by), group))
    for by in (1, 2, 3):
        greet_again((slab, level(by)))

    own_row = owner[...]
    diag = lax.broadcasted_iota(jnp.int32, (32, 32), 0) == lax.broadcasted_iota(jnp.int32, (32, 32), 1)
    own_col = jnp.sum(jnp.where(diag, own_row, 0), axis=1, keepdims=True)
    block_wide = lax.broadcasted_iota(jnp.int32, (32, 128), 0)
    of_lane = lax.broadcasted_iota(jnp.int32, (32, 128), 1) // 4
    own_wide = jnp.sum(jnp.where(block_wide == of_lane, own_col, 0), axis=0, keepdims=True)
    earlier = (own_col == own_wide) & (block_wide < of_lane)
    rank = jnp.sum(jnp.where(earlier, 1, 0), axis=0, keepdims=True)
    relative = own_wide - slab
    relative = jnp.where(relative < 0, relative + slabs, relative)
    key = relative * 16 + rank * 4 + lax.broadcasted_iota(jnp.int32, (1, 128), 1) % 4
    to_slots = onehot(key, 256)
    square = lax.broadcasted_iota(jnp.int32, (128, 128), 0) == lax.broadcasted_iota(jnp.int32, (128, 128), 1)
    key_col = jnp.sum(jnp.where(square, key, 0), axis=1, keepdims=True)

    node = block_nodes[...]
    numbers[...] = jnp.zeros_like(numbers)
    for side in range(2):
        span = slice(128 * side, 128 * side + 128)
        numbers[side, pl.ds(0, 32, stride=4), :] = ((node[:, span] >> 8) + 1).astype(F32)
        numbers[side, pl.ds(1, 32, stride=4), :] = ((node[:, span] & 255) + 1).astype(F32)
    named = jnp.concatenate([numbers[0], numbers[1]], axis=1).astype(BF)
    asks = jnp.dot(to_slots, named, preferred_element_type=F32) - 1.0
    asking[...] = asks.astype(BF).reshape(16, 16, 256)

    def exchange(source, landing, send, recv):
        def copy(q):
            return pltpu.make_async_remote_copy(
                src_ref=source.at[q],
                dst_ref=landing.at[slabs - q],
                send_sem=send.at[q],
                recv_sem=recv.at[slabs - q],
                device_id=(slab_at(q), group),
                device_id_type=MESH,
            )

        def arrival(q):
            return pltpu.make_async_remote_copy(
                src_ref=source.at[q],
                dst_ref=landing.at[q],
                send_sem=send.at[q],
                recv_sem=recv.at[q],
                device_id=(slab_at(q), group),
                device_id_type=MESH,
            )

        return copy, arrival

    def ordered(order, turn, c):
        q = order[c]
        for t in range(1, 3):
            q = jnp.where(turn == t, order[5 * t + c], q)
        return q

    ask_copy, ask_arrival = exchange(asking, asked, ask_send, ask_recv)
    ans_copy, ans_arrival = exchange(answer, answered, ans_send, ans_recv)
    give_copy, give_arrival = exchange(giving, given, give_send, give_recv)

    pl.semaphore_wait(enter_sem, 5)
    for q in FAR:
        ask_copy(q).start()
    asked[0] = asking[0]

    def flatten(quad, carry):
        rows = [cell_nodes[pl.ds(4 * quad + e, 1), :] for e in range(4)]
        nodes[quad] = jnp.concatenate(rows, axis=1)
        return carry

    lax.fori_loop(0, 8, flatten, 0, unroll=4)
    rows_quad = lax.broadcasted_iota(jnp.int32, (128, QUAD), 0)

    def pick(total, row):
        mask = rows_quad == row
        return [
            jnp.sum(jnp.where(mask, total[128 * i : 128 * i + 128], 0.0), axis=0, keepdims=True) for i in range(3)
        ]

    def gather_own(quad, carry):
        number = nodes[quad]
        side_of, row, column = number >> 15, (number >> 8) & 127, number & 255
        for side in range(3):
            columns[quad, side] = onehot(jnp.where(side_of == side, column, -1), 256)
        total = jnp.dot(tables[1], columns[quad, 1], preferred_element_type=F32)
        for i, line in enumerate(pick(total, row)):
            near[quad, i : i + 1, :] = line
        return carry

    lax.fori_loop(0, 8, gather_own, 0, unroll=2)
    load_prev.wait()

    def set_base(i, at, value):
        state[i, at, :] = 2.0 * state[i, at, :] - value

    relaid(prev, set_base)
    def absent(side):
        tables[side] = jnp.zeros((384, 256), BF)

    pl.when(has_below)(to_above.wait_recv)
    pl.when(has_above)(to_below.wait_recv)
    pl.when(slab == 0)(lambda: absent(0))
    pl.when(slab == slabs - 1)(lambda: absent(2))

    def gather_sides(quad, carry):
        row = (nodes[quad] >> 8) & 127
        total = jnp.dot(tables[0], columns[quad, 0], preferred_element_type=F32)
        total += jnp.dot(tables[2], columns[quad, 2], preferred_element_type=F32)
        for i, line in enumerate(pick(total, row)):
            near[quad, i : i + 1, :] += line
        return carry

    lax.fori_loop(0, 8, gather_sides, 0, unroll=4)
    load_grads.wait()
    sub = lax.broadcasted_iota(jnp.int32, (8, 384), 0)
    lane = lax.broadcasted_iota(jnp.int32, (8, 384), 1)
    own = (sub >= 4) == (lane >= 192)

    def gradient(quad, carry):
        for pair in range(2):
            left = jnp.zeros((8, 384), F32)
            for i in range(3):
                left = jnp.where(sub % 4 == i, near[quad, i : i + 1, 384 * pair : 384 * pair + 384], left)
            left = jnp.where(own, left, 0.0).astype(BF)
            for j in range(3):
                first = 4 * quad + 2 * pair
                both = jnp.concatenate([grads[first, j], grads[first + 1, j]], axis=0)
                at = pl.ds(pl.multiple_of(16 * quad + 8 * pair, 8), 8)
                field[j, at, :] = jnp.dot(left, both, preferred_element_type=F32)
        return carry

    lax.fori_loop(0, 8, gradient, 0, unroll=8)
    full = [
        [field[j, pl.ds(i, 32, stride=4), :] + (1.0 if i == j else 0.0) for j in range(3)]
        for i in range(3)
    ]
    cofactor = [
        [
            full[(i + 1) % 3][(j + 1) % 3] * full[(i + 2) % 3][(j + 2) % 3]
            - full[(i + 1) % 3][(j + 2) % 3] * full[(i + 2) % 3][(j + 1) % 3]
            for j in range(3)
        ]
        for i in range(3)
    ]
    volume = full[0][0] * cofactor[0][0] + full[0][1] * cofactor[0][1] + full[0][2] * cofactor[0][2]
    clamped = jnp.maximum(volume, 0.3)
    mu = jnp.sum(jnp.where(diag, shear[...], 0.0), axis=1, keepdims=True)
    lam = jnp.sum(jnp.where(diag, bulk[...], 0.0), axis=1, keepdims=True)
    weight = weights[...]
    factor = (lam * jnp.log(clamped) - mu) / clamped
    for i in range(3):
        for j in range(3):
            field[j, pl.ds(i, 32, stride=4), :] = weight * (mu * full[i][j] + factor * cofactor[i][j])
    low_lane = lax.broadcasted_iota(jnp.int32, (1, 384), 1) < 192
    rows_pair = lax.broadcasted_iota(jnp.int32, (128, 384), 0)

    def cell_forces(quad, carry):
        for pair in range(2):
            total = None
            for j in range(3):
                first = 4 * quad + 2 * pair
                at = pl.ds(pl.multiple_of(16 * quad + 8 * pair, 8), 8)
                both = jnp.concatenate([grads[first, j], grads[first + 1, j]], axis=0)
                piece = lax.dot_general(field[j, at, :].astype(BF), both, NT, preferred_element_type=F32)
                total = piece if total is None else total + piece
            span = slice(384 * pair, 384 * pair + 384)
            mask = rows_pair == ((nodes[quad, :, span] >> 8) & 127)
            for i in range(3):
                value = jnp.where(low_lane, total[i : i + 1], total[4 + i : 5 + i])
                spread[quad, 128 * i : 128 * i + 128, span] = jnp.where(mask, value, 0.0).astype(BF)
        return carry

    lax.fori_loop(0, 8, cell_forces, 0, unroll=8)

    def pair_copy(side):
        return pltpu.make_async_remote_copy(
            src_ref=forces.at[side, :, :, 1 - core],
            dst_ref=paired.at[side],
            send_sem=pair_send.at[side],
            recv_sem=pair_recv.at[side],
            device_id=sibling,
            device_id_type=MESH,
        )

    def force_copy(k):
        source, shift, by = ((0, -1, k), (2, 1, k - 4), (1, 0, k - 7))[k // 4]
        return pltpu.make_async_remote_copy(
            src_ref=merged.at[source, :, depth_at(by)],
            dst_ref=got.at[k],
            send_sem=force_send.at[k],
            recv_sem=force_recv.at[k],
            device_id=(slab_at(shift), level(by)),
            device_id_type=MESH,
        )

    def scatter(side):
        total = None
        for quad in range(8):
            piece = lax.dot_general(spread[quad], columns[quad, side], NT, preferred_element_type=F32)
            total = piece if total is None else total + piece
        for i in range(3):
            forces[side, i] = total[128 * i : 128 * i + 128].reshape(4, 2, 16, 256).astype(BF)
        pair_copy(side).start()

    def merge(side, first, last):
        pair_copy(side).wait_recv()
        for i in range(3):
            merged[side, i] = (forces[side, i, :, core].astype(F32) + paired[side, i].astype(F32)).astype(BF)
        def leave():
            for k in range(first, last):
                force_copy(k).start()

        pl.when((has_below, slab >= 0, has_above)[side])(leave)

    scatter(0)
    scatter(2)
    merge(0, 0, 4)
    scatter(1)
    merge(2, 4, 8)

    def spots(q):
        spot = asked[q].astype(F32)
        row = jnp.concatenate([spot[4 * c : 4 * c + 1] for c in range(CAP)], axis=1).astype(jnp.int32)
        column = jnp.concatenate([spot[4 * c + 1 : 4 * c + 2] for c in range(CAP)], axis=1).astype(jnp.int32)
        return row, column

    def heat(q):
        hots[q] = onehot(spots(q)[1], 256)

    def heat_far(q, carry):
        ask_arrival(q).wait_recv()
        heat(q)
        return carry

    heat(0)
    merge(1, 8, 11)
    lax.fori_loop(1, 16, heat_far, 0, unroll=3)
    for i in range(3):
        goal[pl.ds(i, 32, stride=4), :] = target[i]
    goal[pl.ds(3, 32, stride=4), :] = jnp.zeros((32, 128), F32)
    for i in range(4):
        held[pl.ds(i, 32, stride=4), :] = fixed[...].astype(F32)
    load_phi.wait()
    load_corr.wait()

    def narrow(pair, carry):
        phi_bf[pair] = phi[pair].astype(BF)
        corr_bf[pair] = corr[pair].astype(BF)
        return carry

    lax.fori_loop(0, 16, narrow, 0)
    load_mass.wait()

    pooled[...] = merged[1, :, depth].astype(F32)

    def collect(first, last):
        value = pooled[...]
        for k in range(first, last):
            force_copy(k).wait_recv()
            value = value + got[k].astype(F32)
        pooled[...] = value

    collect(8, 11)
    pl.when(has_above)(lambda: collect(0, 4))
    pl.when(has_below)(lambda: collect(4, 8))

    def shared(buffer, send, recv):
        def copy(by):
            return pltpu.make_async_remote_copy(
                src_ref=buffer.at[:, group],
                dst_ref=buffer.at[:, group],
                send_sem=send.at[by],
                recv_sem=recv.at[groups - by],
                device_id=(slab, group_at(by)),
                device_id_type=MESH,
            )

        def arrival(by):
            return pltpu.make_async_remote_copy(
                src_ref=buffer.at[:, group_at(by)],
                dst_ref=buffer.at[:, group_at(by)],
                send_sem=send.at[by],
                recv_sem=recv.at[by],
                device_id=(slab, group_at(by)),
                device_id_type=MESH,
            )

        def begin():
            for by in (4, 3, 5, 2, 6, 1, 7):
                copy(by).start()

        def finish():
            for by in (1, 7, 2, 6, 3, 5, 4):
                arrival(by).wait_recv()

        def close():
            for by in range(1, groups):
                copy(by).wait_send()

        return begin, finish, close

    sum_begin, sum_finish, sum_close = shared(summed, all_send, all_recv)
    half_begin, half_finish, half_close = shared(halves, half_send, half_recv)
    summed[:, group] = pooled[...].astype(BF)
    sum_begin()
    scale = jnp.concatenate([mass[pl.ds(0, 128, stride=2), :], mass[pl.ds(1, 128, stride=2), :]], axis=1)
    sum_finish()
    for i in range(3):
        state[i] = state[i] - scale * summed[i].reshape(128, 256).astype(F32)
        gathered[128 * i : 128 * i + 128, :] = state[i].astype(BF)

    rows_of = lax.broadcasted_iota(jnp.int32, (128, 1024), 0)
    sixteen = lax.broadcasted_iota(jnp.int32, (16, 256), 0)

    def look(q):
        row, _ = spots(q)
        hit = jnp.dot(gathered[...], hots[q], preferred_element_type=F32)
        mask = rows_of == row
        found = jnp.zeros((16, 256), F32)
        for i in range(3):
            line = jnp.sum(jnp.where(mask, hit[128 * i : 128 * i + 128], 0.0), axis=0, keepdims=True)
            for c in range(CAP):
                found = jnp.where(sixteen == 4 * c + i, line[:, 256 * c : 256 * c + 256], found)
        return found.astype(BF)

    def look_far(turn, carry):
        for c in range(5):
            q = ordered(FAR, turn, c)
            answer[q] = look(q)
            ans_copy(q).start()
        return carry

    lax.fori_loop(0, 3, look_far, 0)
    answered[0] = look(0)
    to_blocks = jnp.where(lax.broadcasted_iota(jnp.int32, (128, 256), 1) == key_col, 1.0, 0.0).astype(BF)

    for q in NEAR:
        ans_arrival(q).wait_recv()
    values[...] = jnp.dot(to_blocks, answered[...].reshape(256, 256), preferred_element_type=F32)

    upper = lax.broadcasted_iota(jnp.int32, (8, 128), 0) < 4

    def at_pair(pair):
        return pl.ds(pl.multiple_of(8 * pair, 8), 8)

    def residual(pair, carry):
        at = at_pair(pair)
        both = lax.dot_general(values[at, :].astype(BF), phi_bf[pair], NT, preferred_element_type=F32)
        interp = jnp.where(upper, both[:, :128], both[:, 128:])
        resids[at, :] = held[at, :] * (goal[at, :] - interp)
        return carry

    def correction(pair, carry):
        at = at_pair(pair)
        both = lax.dot_general(resids[at, :].astype(BF), corr_bf[pair], NT, preferred_element_type=F32)
        values[at, 0:128] = jnp.where(upper, both[:, :128], 0.0)
        values[at, 128:256] = jnp.where(upper, 0.0, both[:, 128:])
        return carry

    def spreading(pair, carry):
        at = at_pair(pair)
        values[at, :] = jnp.dot(values[at, :].astype(BF), phi_bf[pair], preferred_element_type=F32)
        return carry

    lax.fori_loop(0, 16, residual, 0, unroll=16)
    lax.fori_loop(0, 16, correction, 0, unroll=16)
    lax.fori_loop(0, 16, spreading, 0, unroll=16)
    gives = jnp.dot(to_slots, values[...].astype(BF), preferred_element_type=F32).astype(BF)
    giving[...] = gives.reshape(16, 16, 256)
    for q in FAR:
        give_copy(q).start()
    given[0] = giving[0]

    def place(q):
        row, _ = spots(q)
        mask = rows_of == row
        amount = given[q].astype(F32)
        rows = []
        for i in range(3):
            line = jnp.concatenate([amount[4 * c + i : 4 * c + i + 1] for c in range(CAP)], axis=1)
            rows.append(jnp.where(mask, line, 0.0).astype(BF))
        return lax.dot_general(jnp.concatenate(rows, axis=0), hots[q], NT, preferred_element_type=F32)

    adding[...] = place(0)

    def place_far(turn, carry):
        total = None
        for c in range(5):
            q = ordered(NEAR, turn, c)
            give_arrival(q).wait_recv()
            piece = place(q)
            total = piece if total is None else total + piece
        adding[...] += total
        return carry

    lax.fori_loop(0, 3, place_far, 0, unroll=3)
    for i in range(3):
        part[i] = adding[128 * i : 128 * i + 128, :].reshape(8, 16, 256).astype(BF)

    def part_copy(by):
        return pltpu.make_async_remote_copy(
            src_ref=part.at[:, group_at(by)],
            dst_ref=got.at[11 + groups - by],
            send_sem=part_send.at[by],
            recv_sem=part_recv.at[groups - by],
            device_id=(slab, group_at(by)),
            device_id_type=MESH,
        )

    def part_arrival(by):
        return pltpu.make_async_remote_copy(
            src_ref=part.at[:, group_at(by)],
            dst_ref=got.at[11 + by],
            send_sem=part_send.at[by],
            recv_sem=part_recv.at[by],
            device_id=(slab, group_at(by)),
            device_id_type=MESH,
        )

    for by in (4, 3, 5, 2, 6, 1, 7):
        part_copy(by).start()
    share = part[:, group].astype(F32)
    for by in (1, 7, 2, 6, 3, 5, 4):
        part_arrival(by).wait_recv()
        share = share + got[11 + by].astype(F32)
    halves[:, group] = share.astype(BF)
    half_begin()
    half_finish()
    for i in range(3):
        out[i] = state[i] + halves[i].reshape(128, 256).astype(F32)

    def end_far(q, carry):
        ask_copy(q).wait_send()
        ans_copy(q).wait_send()
        give_copy(q).wait_send()
        return carry

    pl.when(has_above)(to_above.wait_send)
    pl.when(has_below)(to_below.wait_send)
    for side in range(3):
        pair_copy(side).wait_send()
    def sent(first, last):
        for k in range(first, last):
            force_copy(k).wait_send()

    pl.when(has_below)(lambda: sent(0, 4))
    pl.when(has_above)(lambda: sent(4, 8))
    sent(8, 11)
    lax.fori_loop(1, 16, end_far, 0)
    sum_close()
    for by in range(1, groups):
        part_copy(by).wait_send()
    half_close()


def body(
    disp_now, disp_prev, inv_mass, cell_nodes, shape_grads, cell_weights, cell_shear, cell_bulk,
    block_owner, block_nodes, block_phi, block_corr, block_target, block_fixed,
):
    vmem = pl.BlockSpec(memory_space=pltpu.VMEM)
    hbm = pl.BlockSpec(memory_space=pltpu.HBM)
    dma = pltpu.SemaphoreType.DMA
    message = pltpu.VMEM((16, 16, 256), BF)
    nodal = pltpu.VMEM((3, 8, 16, 256), BF)
    paired = pltpu.VMEM((3, 3, 4, 16, 256), BF)
    result = pl.pallas_call(
        step_kernel,
        name="step",
        out_shape=jax.ShapeDtypeStruct((3, 128, 256), F32),
        in_specs=[hbm] * 14,
        out_specs=vmem,
        scratch_shapes=[
            pltpu.VMEM((32, 192), jnp.int32),
            pltpu.VMEM((32, 128), F32),
            pltpu.VMEM((1, 32), F32),
            pltpu.VMEM((1, 32), F32),
            pltpu.VMEM((1, 32), jnp.int32),
            pltpu.VMEM((32, 256), jnp.int32),
            pltpu.VMEM((3, 32, 128), F32),
            pltpu.VMEM((32, 128), jnp.int32),
            pltpu.VMEM((3, 32768), F32),
            pltpu.VMEM((3, 32768), F32),
            pltpu.VMEM((256, 128), F32),
            pltpu.VMEM((3, 128, 256), F32),
            pltpu.VMEM((3, 384, 256), BF),
            pltpu.VMEM((8, 1, QUAD), jnp.int32),
            pltpu.VMEM((32, 3, 192, 128), BF),
            pltpu.VMEM((3, 128, 128), F32),
            pltpu.VMEM((8, 8, QUAD), F32),
            pltpu.VMEM((8, 3, 256, QUAD), BF),
            pltpu.VMEM((8, 384, QUAD), BF),
            pltpu.VMEM((3, 3, 4, 2, 16, 256), BF),
            paired,
            paired,
            pltpu.VMEM((3, 16, 256), F32),
            pltpu.VMEM((19, 3, 16, 256), BF),
            nodal,
            message, message, message, message, message, message,
            pltpu.VMEM((384, 256), F32),
            nodal,
            nodal,
            pltpu.VMEM((16, 256, 256), F32),
            pltpu.VMEM((16, 256, 128), F32),
            pltpu.VMEM((16, 256, 256), BF),
            pltpu.VMEM((16, 256, 128), BF),
            pltpu.VMEM((128, 128), F32),
            pltpu.VMEM((128, 128), F32),
            pltpu.VMEM((2, 128, 128), F32),
            pltpu.VMEM((128, 256), F32),
            pltpu.VMEM((128, 128), F32),
            pltpu.VMEM((384, 256), BF),
            pltpu.VMEM((16, 256, 1024), BF),
            dma((14,)), pltpu.SemaphoreType.REGULAR, dma((3,)), dma((3,)), dma((3,)), dma((3,)), dma((11,)), dma((11,)),
            dma((8,)), dma((8,)), dma((16,)), dma((16,)), dma((16,)), dma((16,)), dma((16,)), dma((16,)), dma((8,)),
            dma((8,)), dma((8,)), dma((8,)),
        ],
        compiler_params=pltpu.CompilerParams(
            vmem_limit_bytes=60 << 20, collective_id=0, has_side_effects=True
        ),
    )(
        disp_now,
        disp_prev,
        inv_mass.reshape(256, 128),
        cell_nodes,
        shape_grads,
        cell_weights,
        cell_shear.reshape(1, 32),
        cell_bulk.reshape(1, 32),
        block_owner.reshape(1, 32),
        block_nodes,
        block_phi.reshape(16, 256, 256),
        block_corr.reshape(16, 256, 128),
        jnp.moveaxis(block_target, 1, 0),
        block_fixed,
    )
    return result.reshape(3, 32768)


def solution(mesh):
    both = ("slab", "group")
    placed = (
        P(None, "slab"), P(None, "slab"), P("slab"), P(both, None), P(both, None, None, None), P(both, None),
        P(both), P(both), P(both, None), P(both, None), P(both, None, None), P(both, None, None),
        P(both, None, None), P(both, None),
    )
    return jax.shard_map(body, mesh=mesh, in_specs=placed, out_specs=P(None, "slab"), check_vma=False)
```
